128 devices in a mesh: frames: 16 (over z_lo, x, core), rows: 8 (over z_hi, y).
Axes of the slice: x: 4, y: 4, z: 4 (z_hi: 2, z_lo: 2; z = z_hi * 2 + z_lo), core: 2. Of those that a mesh axis runs over, the one named last changes fastest.
Arguments:
- video: bfloat16 [32, 64, 512, 256], P('frames', 'rows'), may hold values from -36 to 36
- w_time: bfloat16 [3, 256, 256], replicated, may hold values from -0.21875 to 0.21875
- w_proj: bfloat16 [256, 128], replicated, may hold values from -0.375 to 0.375
- w_space: bfloat16 [3, 3, 128, 128], replicated, may hold values from -0.1875 to 0.1875
- gn_gain: float32 [128], replicated, may hold values from 0.1 to 1.9
- gn_bias: float32 [128], replicated, may hold values from -3 to 3
- noise: bfloat16 [64, 64, 512, 128], P(None, 'rows', 'frames'), may hold values from -6 to 6
Outputs:
- sample: bfloat16 [64, 64, 512, 128], P(None, 'rows', 'frames')
The draws below stay inside these ranges and needn't reach their ends.
All inputs are finite; a program needn't handle non-finite values.
Results may differ from the reference program's by a relative error of at most 0.0048.
The reference program's roundings to bfloat16 on the way (of `mixed`, `proj`, `doubled` and `act`) count: a program that leaves them out, or rounds other values in their place, can miss the bound.
Values may be sent and summed in bfloat16 or wider, within the bound.
A program may use at most 192 MiB of HBM per device.

```python
import math
import jax
import jax.numpy as jnp
from jax import lax

C1 = 256
C2 = 128
GROUPS = 32
FRAMES = 32
FRAMES2 = 64
H = 64
W = 512


def draw_video(key, part):
    key = jax.random.fold_in(key, 11)
    first, second, third = jax.random.split(key, 3)
    base = jnp.clip(jax.random.normal(first, (FRAMES, H, W, C1), jnp.float32), -6.0, 6.0)
    spread = math.log(10.0)
    row_scale = 0.2 * jnp.exp(jax.random.uniform(second, (FRAMES, H, 1, 1), jnp.float32) * spread)
    row_scale = jnp.minimum(row_scale, 2.0)
    col_scale = jnp.exp(jax.random.uniform(third, (1, 1, W, 1), jnp.float32) * math.log(1.5))
    ramp = jnp.exp(jnp.arange(H, dtype=jnp.float32).reshape(1, H, 1, 1) / H * math.log(3.0))
    values = base * row_scale * col_scale * ramp / 1.5
    return jnp.clip(values, -36.0, 36.0).astype(jnp.bfloat16)


def block_levels(rng, extent, shards, smallest, largest):
    def one(dim, shards_of):
        heights = jax.random.uniform(jax.random.fold_in(jax.random.fold_in(rng, 6), dim), (shards_of,), jnp.float32, smallest / len(shards), largest / len(shards))
        return jnp.repeat(jnp.exp(heights), extent[dim] // shards_of).reshape((-1,) + (1,) * (len(extent) - dim - 1))

    factor_of = one(*shards[0])
    for cut in shards[1:]:
        factor_of = factor_of * one(*cut)
    return factor_of


def scatter_about(stream_key, shape, scale, reach, pieces=(), kind=jnp.bfloat16):
    entries = scale * jax.random.normal(stream_key, shape, jnp.float32)
    if pieces:
        entries = entries * block_levels(stream_key, shape, pieces, -0.22, 0.18)
    return jnp.clip(entries, -reach, reach).astype(kind)


def setup_inputs(seed: int = 0) -> dict:
    seeds = jax.random.split(jax.random.key(seed), 8)
    video = draw_video(jax.random.fold_in(seeds[7], 71), 0)
    w_time = scatter_about(seeds[1], (3, C1, C1), (3 * C1) ** -0.5, 0.21875)
    w_proj = scatter_about(seeds[2], (C1, C2), C1 ** -0.5, 0.375)
    w_space = scatter_about(seeds[3], (3, 3, C2, C2), (9 * C2) ** -0.5, 0.1875)
    gn_gain = jnp.clip(1.0 + 0.18 * jax.random.normal(seeds[4], (C2,), jnp.float32), 0.1, 1.9)
    gn_bias = scatter_about(seeds[5], (C2,), 0.5, 3.0, (), jnp.float32)
    noise = scatter_about(seeds[6], (FRAMES2, H, W, C2), 1.0, 6.0, ((1, 8), (2, 16)))
    return {"video": video, "w_time": w_time, "w_proj": w_proj, "w_space": w_space, "gn_gain": gn_gain, "gn_bias": gn_bias, "noise": noise}


def double_frames(proj):
    following = jnp.concatenate([proj[1:], proj[-1:]], 0)
    middle = ((proj.astype(jnp.float32) + following.astype(jnp.float32)) * 0.5).astype(jnp.bfloat16)
    count = proj.shape[0]
    return jnp.stack([proj, middle], 1).reshape((2 * count,) + proj.shape[1:])

def reference(video, w_time, w_proj, w_space, gn_gain, gn_bias, noise):
    padded = jnp.pad(video, ((1, 1), (0, 0), (0, 0), (0, 0)))

    def one_frame(index):
        slab = lax.dynamic_slice_in_dim(padded, index, 3, 0)
        taps = jnp.zeros((H, W, C1), jnp.float32)
        for k in range(3):
            taps = taps + jnp.dot(slab[k].reshape(-1, C1), w_time[k], preferred_element_type=jnp.float32).reshape(H, W, C1)
        mixed = (slab[1].astype(jnp.float32) + jax.nn.silu(taps)).astype(jnp.bfloat16)
        return jnp.dot(mixed.reshape(-1, C1), w_proj, preferred_element_type=jnp.float32).reshape(H, W, C2).astype(jnp.bfloat16)
    proj = lax.map(one_frame, jnp.arange(FRAMES, dtype=jnp.int32))
    doubled = double_frames(proj)
    count = H * W * (C2 // GROUPS)

    def one_out(pair):
        frame, shake = pair
        field = frame.astype(jnp.float32)
        grouped = field.reshape(H * W, GROUPS, C2 // GROUPS)
        total = lax.optimization_barrier(jnp.sum(grouped, axis=(0, 2)))
        squares = lax.optimization_barrier(jnp.sum(grouped * grouped, axis=(0, 2)))
        mean = total / count
        var = squares / count - mean * mean
        normed = (grouped - mean[None, :, None]) / jnp.sqrt(var[None, :, None] + 1e-05)
        normed = normed.reshape(H, W, C2) * gn_gain + gn_bias
        act = jax.nn.silu(normed).astype(jnp.bfloat16)
        edged = jnp.pad(act, ((1, 1), (1, 1), (0, 0)))
        result = field + 0.3 * shake.astype(jnp.float32)
        for i in range(3):
            for j in range(3):
                tap = edged[i:i + H, j:j + W].reshape(-1, C2)
                result = result + jnp.dot(tap, w_space[i, j], preferred_element_type=jnp.float32).reshape(H, W, C2)
        return result.astype(jnp.bfloat16)
    return lax.map(one_out, (doubled, noise))
```

```python
import jax
import jax.numpy as jnp
from jax import lax
from jax.experimental import pallas as pl
from jax.experimental.pallas import tpu as pltpu
from jax.sharding import PartitionSpec as P

MESH = pl.DeviceIdType.MESH
HIGH = lax.Precision.HIGHEST
NF, NR = 16, 8
GROUPS = 32
BF, F32 = jnp.bfloat16, jnp.float32

PEERS = [(dz, dx, dc) for dx in (2, 1, 3, 0) for dz in (1, 0) for dc in (0, 1) if (dz, dx, dc) != (0, 0, 0)]


def peer(f, k):
    dz, dx, dc = PEERS[k]
    z, x, c = f // 8, (f // 2) % 4, f % 2
    return ((z + dz) % 2) * 8 + ((x + dx) % 4) * 2 + (c + dc) % 2


def silu(v):
    h = 0.5 * v
    return h + h * jnp.tanh(h)


def group_matrix(k, expand):
    a = lax.broadcasted_iota(jnp.int32, (128, 128), 1 if expand else 0)
    b = lax.broadcasted_iota(jnp.int32, (128, 128), 0 if expand else 1)
    return jnp.where(b == 32 * k + (a >> 2), 1.0, 0.0).astype(F32)


def move_kernel(
    video, wt, wp, pb_out, tb_out, ed_out, st_out,
    vb, pb, tb, eo, ed, st, s1, r1, s2, r2,
    lsem, vs, vr, hs, hr, es, er, as_, ar, bs, br, osem,
):
    f, r = lax.axis_index("frames"), lax.axis_index("rows")
    frames = vb.shape[0] - 2
    barrier = pltpu.get_barrier_semaphore()
    for k in range(NF - 1):
        pl.semaphore_signal(barrier, inc=1, device_id={"frames": peer(f, k)}, device_id_type=MESH)
    for k in range(1, NR):
        pl.semaphore_signal(barrier, inc=1, device_id={"rows": (r + k) % NR}, device_id_type=MESH)
    mine = pltpu.make_async_copy(video.at[:, :, pl.ds(pl.multiple_of(f * 32, 32), 32)], vb.at[pl.ds(1 + 2 * f, 2)], lsem)
    mine.start()
    vb[0] = jnp.zeros(vb.shape[1:], BF)
    vb[frames + 1] = jnp.zeros(vb.shape[1:], BF)
    pl.semaphore_wait(barrier, NF + NR - 2)

    sends = []
    for k in range(NF - 1):
        d = peer(f, k)
        cp = pltpu.make_async_remote_copy(
            src_ref=video.at[:, :, pl.ds(pl.multiple_of(d * 32, 32), 32)],
            dst_ref=vb.at[pl.ds(1 + 2 * f, 2)],
            send_sem=vs.at[k], recv_sem=vr.at[k],
            device_id={"frames": d}, device_id_type=MESH,
        )
        cp.start()
        sends.append(cp)
    mine.wait()
    for cp in sends:
        cp.wait()

    def temporal(t, carry):
        taps = jnp.dot(vb[t].reshape(256, 256), wt[0], preferred_element_type=F32)
        taps += jnp.dot(vb[t + 1].reshape(256, 256), wt[1], preferred_element_type=F32)
        taps += jnp.dot(vb[t + 2].reshape(256, 256), wt[2], preferred_element_type=F32)
        mixed = (vb[t + 1].reshape(256, 256).astype(F32) + silu(taps)).astype(BF)
        pb[t] = jnp.dot(mixed, wp[...], preferred_element_type=F32).astype(BF).reshape(8, 32, 128)
        return carry

    lax.fori_loop(0, frames, temporal, 0, unroll=2)

    rows_up = pltpu.make_async_remote_copy(
        src_ref=pb.at[:, 0], dst_ref=tb.at[1], send_sem=hs.at[0], recv_sem=hr.at[0],
        device_id={"rows": (r + NR - 1) % NR}, device_id_type=MESH)
    rows_down = pltpu.make_async_remote_copy(
        src_ref=pb.at[:, 7], dst_ref=tb.at[0], send_sem=hs.at[1], recv_sem=hr.at[1],
        device_id={"rows": (r + 1) % NR}, device_id_type=MESH)
    rows_up.start()
    rows_down.start()
    pb_copy = pltpu.make_async_copy(pb, pb_out, osem.at[0])
    pb_copy.start()

    def sums(t, carry):
        now = pb[t].reshape(256, 128).astype(F32)
        nxt = pb[jnp.minimum(t + 1, frames - 1)].reshape(256, 128).astype(F32)
        mid = ((now + nxt) * 0.5).astype(BF).astype(F32)
        st[0, pl.ds(2 * t, 1)] = jnp.sum(now, axis=0, keepdims=True)
        st[0, pl.ds(2 * t + 1, 1)] = jnp.sum(mid, axis=0, keepdims=True)
        st[1, pl.ds(2 * t, 1)] = jnp.sum(now * now, axis=0, keepdims=True)
        st[1, pl.ds(2 * t + 1, 1)] = jnp.sum(mid * mid, axis=0, keepdims=True)
        return carry

    lax.fori_loop(0, frames, sums, 0, unroll=2)
    packed = jnp.zeros((32, 128), F32)
    for k in range(4):
        part = st[k // 2, 32 * (k % 2):32 * (k % 2) + 32]
        packed += jnp.dot(part, group_matrix(k, False), precision=HIGH, preferred_element_type=F32)
    s1[...] = packed
    first = []
    for k in range(1, NR):
        cp = pltpu.make_async_remote_copy(
            src_ref=s1, dst_ref=r1.at[k - 1], send_sem=as_.at[k - 1], recv_sem=ar.at[k - 1],
            device_id={"rows": (r + k) % NR}, device_id_type=MESH)
        cp.start()
        first.append(cp)

    rows_up.wait()
    rows_down.wait()
    row = lax.broadcasted_iota(jnp.int32, (32, 256), 0)
    col = lax.broadcasted_iota(jnp.int32, (32, 256), 1)
    wanted = ((row & 15) - 1) * 32 + jnp.where(row >= 16, 31, 0)
    pick = jnp.where((col == wanted) & ((row & 15) >= 1) & ((row & 15) <= 8), 1.0, 0.0).astype(BF)
    row, col = row[:, :64], col[:, :64]
    side = jnp.where(row >= 16, 31, 0)
    pick_tb = jnp.where(((row & 15) == 0) & (col == side) | ((row & 15) == 9) & (col == 32 + side), 1.0, 0.0).astype(BF)

    def edges(t, carry):
        e = jnp.dot(pick, pb[t].reshape(256, 128), preferred_element_type=F32)
        e += jnp.dot(pick_tb[:, :32], tb[0, t], preferred_element_type=F32)
        e += jnp.dot(pick_tb[:, 32:], tb[1, t], preferred_element_type=F32)
        eo[0, t] = e[:16].astype(BF)
        eo[1, t] = e[16:].astype(BF)
        return carry

    lax.fori_loop(0, frames, edges, 0, unroll=2)
    to_left = pltpu.make_async_remote_copy(
        src_ref=eo.at[0], dst_ref=ed.at[1], send_sem=es.at[0], recv_sem=er.at[0],
        device_id={"frames": (f + NF - 1) % NF}, device_id_type=MESH)
    to_right = pltpu.make_async_remote_copy(
        src_ref=eo.at[1], dst_ref=ed.at[0], send_sem=es.at[1], recv_sem=er.at[1],
        device_id={"frames": (f + 1) % NF}, device_id_type=MESH)
    to_left.start()
    to_right.start()
    tb_copy = pltpu.make_async_copy(tb, tb_out, osem.at[1])
    tb_copy.start()

    for cp in first:
        cp.wait()
    total = s1[...]
    for k in range(NR - 1):
        total += r1[k]
    s2[...] = total
    second = []
    for k in range(NF - 1):
        cp = pltpu.make_async_remote_copy(
            src_ref=s2, dst_ref=r2.at[k], send_sem=bs.at[k], recv_sem=br.at[k],
            device_id={"frames": peer(f, k)}, device_id_type=MESH)
        cp.start()
        second.append(cp)
    to_left.wait()
    to_right.wait()
    ed_copy = pltpu.make_async_copy(ed, ed_out, osem.at[2])
    ed_copy.start()
    for cp in second:
        cp.wait()
    for k in range(NF - 1):
        total += r2[k]
    count = 64 * 512 * 4
    for k in range(2):
        mean = jnp.dot(total, group_matrix(k, True), precision=HIGH, preferred_element_type=F32) / count
        square = jnp.dot(total, group_matrix(k + 2, True), precision=HIGH, preferred_element_type=F32) / count
        st_out[0, 32 * k:32 * k + 32] = mean
        st_out[1, 32 * k:32 * k + 32] = lax.rsqrt(square - mean * mean + 1e-05)
    pb_copy.wait()
    tb_copy.wait()
    ed_copy.wait()


def conv_kernel(pb, tb, ed, st, ws, gain, bias, noise, out, w0, w1, ll, ea, fld):
    f, r = lax.axis_index("frames"), lax.axis_index("rows")
    g = pl.program_id(0)
    last = pb.shape[0] - 1
    half = noise.shape[0] // 2

    @pl.when(g == 0)
    def _():
        zero = jnp.zeros((128, 128), BF)
        for j in range(3):
            for a in range(2):
                for b in range(2):
                    i = a - b
                    at = (slice(256 * j + 128 * a, 256 * j + 128 * a + 128), slice(128 * b, 128 * b + 128))
                    w0[at] = ws[i, j] if 0 <= i else zero
                    i = 2 + a - b
                    w1[at] = ws[i, j] if i <= 2 else zero

    keep_top = jnp.where(r > 0, 1.0, 0.0)
    keep_bottom = jnp.where(r < NR - 1, 1.0, 0.0)
    keep_side = (jnp.where(f > 0, 1.0, 0.0), jnp.where(f < NF - 1, 1.0, 0.0))
    sub = lax.broadcasted_iota(jnp.int32, (32, 128), 0)

    def one(n, carry):
        t = g * half + n
        u = jnp.minimum(t + 1, last)
        for odd in range(2):
            mean = st[0, pl.ds(2 * t + odd, 1)]
            scale = 0.5 * (st[1, pl.ds(2 * t + odd, 1)] * gain[...])
            shift = 0.5 * bias[...]

            def field_of(ref, *at):
                v = ref[at[0] + (t,) + at[1]].astype(F32)
                if odd:
                    v = ((v + ref[at[0] + (u,) + at[1]].astype(F32)) * 0.5).astype(BF).astype(F32)
                return v

            def act_of(v):
                h = (v - mean) * scale + shift
                return h + h * jnp.tanh(h)

            for s in range(2):
                ea[s] = act_of(field_of(ed, (s,), ())) * keep_side[s]
            for R in range(10):
                if R == 0:
                    a = act_of(field_of(tb, (0,), ())) * keep_top
                elif R == 9:
                    a = act_of(field_of(tb, (1,), ())) * keep_bottom
                else:
                    v = field_of(pb, (), (R - 1,))
                    fld[2 * n + odd, R - 1] = v
                    a = act_of(v)
                el, er = ea[0, R:R + 1], ea[1, R:R + 1]
                if R == 0:
                    el, er = el * keep_top, er * keep_top
                if R == 9:
                    el, er = el * keep_bottom, er * keep_bottom
                before = jnp.where(sub == 0, el, pltpu.roll(a, 1, 0))
                after = jnp.where(sub == 31, er, pltpu.roll(a, 31, 0))
                place = pl.ds(pl.multiple_of((2 * n + odd) * 32, 32), 32)
                for j, v in enumerate((before, a, after)):
                    lane = 256 * j + 128 * (R % 2)
                    ll[R // 2, place, lane:lane + 128] = v.astype(BF)
        return carry

    lax.fori_loop(0, half, one, 0)
    count = 2 * half
    for p in range(4):
        res = jnp.dot(ll[p], w0[...], preferred_element_type=F32)
        res += jnp.dot(ll[p + 1], w1[...], preferred_element_type=F32)
        for b in range(2):
            R = 2 * p + b
            v = res[:, 128 * b:128 * b + 128].reshape(count, 32, 128)
            out[:, R] = (v + fld[:, R] + 0.3 * noise[:, R].astype(F32)).astype(BF)


def local(video, w_time, w_proj, w_space, gn_gain, gn_bias, noise):
    frames = 2 * NF
    full = lambda shape: pl.BlockSpec(shape, lambda g: (0,) * len(shape))
    anyw = pl.BlockSpec(memory_space=pl.ANY)
    vm = pl.BlockSpec(memory_space=pltpu.VMEM)
    pb, tb, ed, st = pl.pallas_call(
        move_kernel,
        out_shape=(
            jax.ShapeDtypeStruct((frames, 8, 32, 128), BF),
            jax.ShapeDtypeStruct((2, frames, 32, 128), BF),
            jax.ShapeDtypeStruct((2, frames, 16, 128), BF),
            jax.ShapeDtypeStruct((2, 64, 128), F32),
        ),
        in_specs=[anyw, vm, vm],
        out_specs=(anyw, anyw, anyw, vm),
        scratch_shapes=[
            pltpu.VMEM((frames + 2, 8, 32, 256), BF),
            pltpu.VMEM((frames, 8, 32, 128), BF),
            pltpu.VMEM((2, frames, 32, 128), BF),
            pltpu.VMEM((2, frames, 16, 128), BF),
            pltpu.VMEM((2, frames, 16, 128), BF),
            pltpu.VMEM((2, 64, 128), F32),
            pltpu.VMEM((32, 128), F32),
            pltpu.VMEM((NR - 1, 32, 128), F32),
            pltpu.VMEM((32, 128), F32),
            pltpu.VMEM((NF - 1, 32, 128), F32),
            pltpu.SemaphoreType.DMA,
            pltpu.SemaphoreType.DMA((NF - 1,)),
            pltpu.SemaphoreType.DMA((NF - 1,)),
            pltpu.SemaphoreType.DMA((2,)),
            pltpu.SemaphoreType.DMA((2,)),
            pltpu.SemaphoreType.DMA((2,)),
            pltpu.SemaphoreType.DMA((2,)),
            pltpu.SemaphoreType.DMA((NR - 1,)),
            pltpu.SemaphoreType.DMA((NR - 1,)),
            pltpu.SemaphoreType.DMA((NF - 1,)),
            pltpu.SemaphoreType.DMA((NF - 1,)),
            pltpu.SemaphoreType.DMA((3,)),
        ],
        compiler_params=pltpu.CompilerParams(collective_id=0, has_side_effects=True, vmem_limit_bytes=40 << 20),
        name="move",
    )(video, w_time, w_proj)

    per = 8
    return pl.pallas_call(
        conv_kernel,
        grid=(64 // per,),
        out_shape=jax.ShapeDtypeStruct((64, 8, 32, 128), BF),
        in_specs=[
            full((frames, 8, 32, 128)), full((2, frames, 32, 128)), full((2, frames, 16, 128)), full((2, 64, 128)),
            full((3, 3, 128, 128)), full((1, 128)), full((1, 128)),
            pl.BlockSpec((per, 8, 32, 128), lambda g: (g, 0, 0, 0)),
        ],
        out_specs=pl.BlockSpec((per, 8, 32, 128), lambda g: (g, 0, 0, 0)),
        scratch_shapes=[
            pltpu.VMEM((768, 256), BF),
            pltpu.VMEM((768, 256), BF),
            pltpu.VMEM((5, per * 32, 768), BF),
            pltpu.VMEM((2, 16, 128), F32),
            pltpu.VMEM((per, 8, 32, 128), F32),
        ],
        compiler_params=pltpu.CompilerParams(vmem_limit_bytes=40 << 20),
        name="conv",
    )(pb, tb, ed, st, w_space, gn_gain.reshape(1, 128), gn_bias.reshape(1, 128), noise)


def solution(mesh):
    in_specs = (
        P("frames", "rows", None, None),
        P(), P(), P(), P(), P(),
        P(None, "rows", "frames", None),
    )
    out_specs = P(None, "rows", "frames", None)
    return jax.shard_map(local, mesh=mesh, in_specs=in_specs, out_specs=out_specs, check_vma=False)
```

```python
import jax
import jax.numpy as jnp
from jax import lax
from jax.experimental import pallas as pl
from jax.experimental.pallas import tpu as pltpu
from jax.sharding import PartitionSpec as P

MESH = pl.DeviceIdType.MESH
NF, NR = 16, 8
GROUPS = 32
BF, F32 = jnp.bfloat16, jnp.float32

PEERS = [(dz, dx, dc) for dx in (2, 1, 3, 0) for dz in (1, 0) for dc in (0, 1) if (dz, dx, dc) != (0, 0, 0)]


def peer(f, k):
    dz, dx, dc = PEERS[k]
    z, x, c = f // 8, (f // 2) % 4, f % 2
    return ((z + dz) % 2) * 8 + ((x + dx) % 4) * 2 + (c + dc) % 2


def silu(v):
    h = 0.5 * v
    return h + h * jnp.tanh(h)


def gather_groups(parts):
    lane = lax.broadcasted_iota(jnp.int32, parts[0].shape, 1) & 3
    out = jnp.zeros(parts[0].shape, F32)
    for k, v in enumerate(parts):
        v = v + pltpu.roll(v, 127, 1)
        v = v + pltpu.roll(v, 126, 1)
        out = jnp.where(lane == k, pltpu.roll(v, k, 1) if k else v, out)
    return out


def spread_groups(v, k):
    lane = lax.broadcasted_iota(jnp.int32, v.shape, 1) & 3
    v = jnp.where(lane == k, v, 0.0)
    v = pltpu.roll(v, 128 - k, 1) if k else v
    v = v + pltpu.roll(v, 1, 1)
    return v + pltpu.roll(v, 2, 1)


def temporal(before, now, after, w3, wp):
    x = [v.reshape(512, 256) for v in (before, now, after)]
    taps = jnp.dot(jnp.concatenate(x, axis=1), w3[...], preferred_element_type=F32)
    mixed = (x[1].astype(F32) + silu(taps)).astype(BF)
    proj = jnp.dot(mixed, wp[...], preferred_element_type=F32).astype(BF)
    return proj.reshape(8, 2, 32, 128)


def border_keeps(f, r):
    return (jnp.where(r > 0, 1.0, 0.0), jnp.where(r < NR - 1, 1.0, 0.0),
            (jnp.where(f > 0, 1.0, 0.0), jnp.where(f < NF - 1, 1.0, 0.0)))


def norm_frame(now, nxt, line, place, pb, tb, ed, st, gain, bias, ea, ll, fld, keeps):
    keep_top, keep_bottom, keep_side = keeps
    line = pl.ds(line, 1)
    scale = st[1, line] * gain[...]
    shift = 0.5 * (bias[...] - st[0, line] * scale)
    scale = (0.5 if nxt is None else 0.25) * scale
    sub = lax.broadcasted_iota(jnp.int32, (8, 128), 0)

    def act_of(ref, before, after, keep=None):
        v = ref[before + now + after]
        if nxt is not None:
            v = v + ref[before + nxt + after]
        if keep is not None:
            keep[...] = v
        h = v.astype(F32) * scale + shift
        return h + h * jnp.tanh(h)

    for s in range(2):
        ea[s] = act_of(ed, (s,), ()) * keep_side[s]
    for R in range(10):
        E = 8 if R == 0 else R - 1 if R < 9 else 9
        el, er = ea[0, E:E + 1], ea[1, E:E + 1]
        if R == 0:
            a = act_of(tb, (0,), ()) * keep_top
            el, er = el * keep_top, er * keep_top
        elif R == 9:
            a = act_of(tb, (1,), ()) * keep_bottom
            el, er = el * keep_bottom, er * keep_bottom
        else:
            a = act_of(pb, (), (R - 1,), None if fld is None else fld.at[place, R - 1])
        tiles = [a[8 * i:8 * i + 8] for i in range(4)]
        down = [pltpu.roll(v, 1, 0) for v in tiles]
        up = [pltpu.roll(v, 7, 0) for v in tiles]
        left = [jnp.where(sub == 0, down[i - 1] if i else el, down[i]) for i in range(4)]
        right = [jnp.where(sub == 7, up[i + 1] if i < 3 else er, up[i]) for i in range(4)]
        for j, v in enumerate((jnp.concatenate(left, 0), a, jnp.concatenate(right, 0))):
            lane = 256 * j + 128 * (R % 2)
            ll[R // 2, 32 * place:32 * place + 32, lane:lane + 128] = v.astype(BF)


def fill_weights(ws, w0, w1):
    zero = jnp.zeros((128, 128), BF)
    for j in range(3):
        for a in range(2):
            for b in range(2):
                i = a - b
                at = (slice(256 * j + 128 * a, 256 * j + 128 * a + 128), slice(128 * b, 128 * b + 128))
                w0[at] = ws[i, j] if 0 <= i else zero
                i = 2 + a - b
                w1[at] = ws[i, j] if i <= 2 else zero


def conv_rows(count, ll, w0, w1):
    m = 32 * count
    sides = jnp.concatenate([ll[0:4].reshape(4 * m, 768), ll[1:5].reshape(4 * m, 768)], axis=1)
    res = jnp.dot(sides, jnp.concatenate([w0[...], w1[...]], axis=0), preferred_element_type=F32)
    return [res[m * (R // 2):m * (R // 2) + m, 128 * (R % 2):128 * (R % 2) + 128].reshape(count, 32, 128)
            for R in range(8)]


def conv_kernel(pb, tb, ed, st, early, ws, gain, bias, noise, out, w0, w1, ll_a, ll_b, fld_a, fld_b, ea):
    f, r = lax.axis_index("frames"), lax.axis_index("rows")
    g = pl.program_id(0)
    steps = pl.num_programs(0) - 1
    keeps = border_keeps(f, r)

    @pl.when(g == 0)
    def _():
        fill_weights(ws, w0, w1)

    def step(new, old):
        if new is not None:
            ll, fld = new
            for i, (_, at, nxt) in enumerate(LATE):
                norm_frame(slot_of(g, at), nxt and slot_of(g, nxt), L_ROWS * g + i, i,
                           pb, tb, ed, st, gain, bias, ea.at[i], ll, fld, keeps)
        if old is not None:
            ll, fld = old
            rows = conv_rows(len(LATE), ll, w0, w1)
            for R in range(8):
                for i, (k, _, nxt) in enumerate(LATE):
                    v = fld[i, R].astype(F32) * (1.0 if nxt is None else 0.5)
                    out[k, R] = (rows[R][i] + v + 0.3 * noise[k, R].astype(F32)).astype(BF)
            for i, (k, _, _) in enumerate(EARLY):
                out[k] = early[0, i]

    a, b = (ll_a, fld_a), (ll_b, fld_b)

    @pl.when(g == 0)
    def _():
        step(a, None)

    @pl.when((g > 0) & (g < steps) & (g % 2 == 0))
    def _():
        step(a, b)

    @pl.when((g < steps) & (g % 2 == 1))
    def _():
        step(b, a)

    @pl.when(g == steps)
    def _():
        step(None, b)


EARLY = ((2, (0, 2), None), (3, (0, 2), (0, 3)), (4, (0, 3), None))
LATE = ((0, (0, 1), None), (1, (0, 1), (0, 2)), (5, (0, 3), (1, 0)), (6, (1, 0), None), (7, (1, 0), (1, 1)))
HALO_AT = ((0, 1), (2, 3))
E_ROWS, L_ROWS = 4, 6


def slot_of(q, at):
    if at == (1, 1):
        return q + 1, jnp.where(q == 7, 0, 1)
    return q + at[0], at[1]


def move_kernel(
    video, wt, wp, ws, gain, bias, noise, pb_out, tb_out, ed_out, st_out, early_out,
    vv, inner, halo, relay, w3, si, so, pb, tb, eo, ed,
    st_e, s1e, r1e, s2e, r2e, stat_e, st_l, s1l, r1l, s2l, r2l,
    nz, w0, w1, ll, ea, res_e,
    lsem, ns, nr, hs, hr, ls, lr, is_, ir, os, or_, ts, tr, es, er, sem_e1, sem_e2, sem_l1, sem_l2, osem,
):
    f, r = lax.axis_index("frames"), lax.axis_index("rows")
    z, x, c = f // 8, (f // 2) % 4, f % 2
    chip = f // 2
    sgn = 2 * c - 1
    is_end = (f == 0) | (f == NF - 1)
    not_end = jnp.logical_not(is_end)
    outer_frame, inner_frame = c, 1 - c
    outer_dev = jnp.clip(f + sgn, 0, NF - 1)
    inner_dev = f + 1 - 2 * c

    def wait_in(ref, sem):
        pltpu.make_async_copy(ref, ref, sem).wait()

    def column(zz, xx):
        return pl.ds(pl.multiple_of(zz * 256 + xx * 64, 64), 64)

    def far_first(i):
        j = i // 2
        dx = jnp.where(j == 0, 2, jnp.where(j == 1, 1, jnp.where(j == 2, 3, 0)))
        return (z + 1 - i % 2) % 2, (x + dx) % 4

    def near_first(n, zz, xx, sg):
        dx = jnp.where(n < 4, jnp.where(n % 2 == 0, -sg, 0), jnp.where(n % 2 == 0, sg, 2 * sg))
        return (zz + 1 - (n // 2) % 2) % 2, (xx + dx + 4) % 4

    barrier = pltpu.get_barrier_semaphore()
    for k in range(NF - 1):
        pl.semaphore_signal(barrier, inc=1, device_id={"frames": peer(f, k)}, device_id_type=MESH)
    for k in range(1, NR):
        pl.semaphore_signal(barrier, inc=1, device_id={"rows": (r + k) % NR}, device_id_type=MESH)
    nz_load = pltpu.make_async_copy(noise.at[:, pl.ds(2, 3)], nz, osem.at[4])
    nz_load.start()
    loads = [pltpu.make_async_copy(video.at[k], vv.at[k], lsem.at[k]) for k in range(2)]
    for cp in loads:
        cp.start()
    w3[0:256] = wt[2 - 2 * c]
    w3[256:512] = wt[1]
    w3[512:768] = wt[2 * c]

    @pl.when(is_end)
    def _():
        halo[...] = jnp.zeros(halo.shape, BF)

    for axis_at, ref in ((r, tb), (f, ed)):
        count = NR if ref is tb else NF
        for side, edge in ((0, 0), (1, count - 1)):
            @pl.when(axis_at == edge)
            def _():
                ref[side] = jnp.zeros(ref.shape[1:], BF)

    st_e[...] = jnp.zeros(st_e.shape, F32)
    st_l[...] = jnp.zeros(st_l.shape, F32)
    pl.semaphore_wait(barrier, NF + NR - 2)

    is_mid = (f == NF // 2 - 1) | (f == NF // 2)

    def halo_copy(n):
        zz, xx = near_first(n, outer_dev // 8, (x + sgn + 4) % 4, -sgn)
        return pltpu.make_async_remote_copy(
            src_ref=video.at[:, :, column(zz, xx)], dst_ref=halo.at[n], send_sem=hs.at[n], recv_sem=hr.at[n],
            device_id={"frames": outer_dev}, device_id_type=MESH)

    def detour_copy(n):
        zz, xx = near_first(n, outer_dev // 8, (x + sgn + 4) % 4, -sgn)
        return pltpu.make_async_remote_copy(
            src_ref=video.at[:, :, column(zz, xx)], dst_ref=relay.at[n - 2], send_sem=ls.at[n - 2], recv_sem=lr.at[n - 2],
            device_id={"frames": jnp.where(f < NF // 2, NF - 1, 0)}, device_id_type=MESH)

    def relay_copy(n):
        return pltpu.make_async_remote_copy(
            src_ref=relay.at[n - 2], dst_ref=halo.at[n], send_sem=hs.at[n], recv_sem=hr.at[n],
            device_id={"frames": jnp.where(f < NF // 2, NF // 2 - 1, NF // 2)}, device_id_type=MESH)

    def inner_copy(i):
        zz, xx = far_first(i)
        return pltpu.make_async_remote_copy(
            src_ref=video.at[inner_frame, :, column(zz, xx)], dst_ref=inner.at[i], send_sem=ns.at[i], recv_sem=nr.at[i],
            device_id={"frames": inner_dev}, device_id_type=MESH)

    for i in range(8):
        inner_copy(i).start()

    def halo_start(blocks):
        for n in blocks:
            if n < 2:
                @pl.when(not_end)
                def _():
                    halo_copy(n).start()
            else:
                @pl.when(not_end & jnp.logical_not(is_mid))
                def _():
                    halo_copy(n).start()

    @pl.when(is_mid)
    def _():
        for n in (2, 3):
            detour_copy(n).start()

    halo_start(HALO_AT[0])

    for cp in loads:
        cp.wait()

    def inner_send(i, dc):
        zz, xx = far_first(i)
        dest = zz * 8 + xx * 2 + (c + dc) % 2
        slot = 2 * i + dc
        return pltpu.make_async_remote_copy(
            src_ref=si.at[i, (c + dc) % 2], dst_ref=pb.at[chip, 2 + c], send_sem=is_.at[slot], recv_sem=ir.at[slot],
            device_id={"frames": dest}, device_id_type=MESH)

    def inner_block(i, carry):
        zz, xx = far_first(i)
        wait_in(inner.at[i], nr.at[i])
        here = column(zz, xx)
        proj = temporal(inner[i], vv[inner_frame, :, here], vv[outer_frame, :, here], w3, wp)
        for h in range(2):
            si[i, h] = proj[:, h]
        inner_send(i, 1).start()

        @pl.when(i < 7)
        def _():
            inner_send(i, 0).start()

        return carry

    lax.fori_loop(0, 8, inner_block, 0)
    own_inner = pltpu.make_async_copy(si.at[7, c], pb.at[chip, 2 + c], lsem.at[0])
    own_inner.start()

    def outer_send(n, dc):
        zz, xx = near_first(n, z, x, sgn)
        dest = zz * 8 + xx * 2 + (c + dc) % 2
        slot = 2 * n + dc
        return pltpu.make_async_remote_copy(
            src_ref=so.at[n, (c + dc) % 2], dst_ref=pb.at[chip + c, pl.ds(0, 2)], send_sem=os.at[slot], recv_sem=or_.at[slot],
            device_id={"frames": dest}, device_id_type=MESH)

    def outer_block(n, carry):
        zz, xx = near_first(n, z, x, sgn)
        here = column(zz, xx)
        at = n % 4

        @pl.when(not_end)
        def _():
            wait_in(halo.at[at], hr.at[at])

        proj = temporal(vv[inner_frame, :, here], vv[outer_frame, :, here], halo[at, 1 - c], w3, wp)
        for h in range(2):
            so[n, h, 1 - c] = proj[:, h]
        proj = temporal(vv[outer_frame, :, here], halo[at, 1 - c], halo[at, c], w3, wp)
        for h in range(2):
            so[n, h, c] = proj[:, h]
        outer_send(n, 1).start()

        @pl.when(n != 3)
        def _():
            outer_send(n, 0).start()

        return carry

    def outer_blocks(first, past):
        lax.fori_loop(first, past, outer_block, 0)

    halo_start(HALO_AT[1])

    @pl.when(is_end)
    def _():
        outer_blocks(4, 8)
        outer_blocks(0, 4)
        for n in (2, 3):
            wait_in(relay.at[n - 2], lr.at[n - 2])
            relay_copy(n).start()

    def blocks_not_end(first, past):
        @pl.when(not_end)
        def _():
            outer_blocks(first, past)

    blocks_not_end(0, 2)

    def both_ways(axis, at, up_refs, down_refs, ssem, rsem, base, act):
        count = lax.axis_size(axis)
        first, last = at == 0, at == count - 1
        up = pltpu.make_async_remote_copy(
            src_ref=up_refs[0], dst_ref=up_refs[1], send_sem=ssem.at[base], recv_sem=rsem.at[base],
            device_id={axis: jnp.maximum(at - 1, 0)}, device_id_type=MESH)
        down = pltpu.make_async_remote_copy(
            src_ref=down_refs[0], dst_ref=down_refs[1], send_sem=ssem.at[base + 1], recv_sem=rsem.at[base + 1],
            device_id={axis: jnp.minimum(at + 1, count - 1)}, device_id_type=MESH)

        @pl.when(jnp.logical_not(first))
        def _():
            if act == "start":
                up.start()
            else:
                up.wait_send()
                down.wait_recv()

        @pl.when(jnp.logical_not(last))
        def _():
            if act == "start":
                down.start()
            else:
                down.wait_send()
                up.wait_recv()

    def rows_copies(q, lo, base, act):
        part = (pl.ds(0, q), pl.ds(lo, 2))
        both_ways("rows", r, (pb.at[part + (0,)], tb.at[(1,) + part]), (pb.at[part + (7,)], tb.at[(0,) + part]), ts, tr, base, act)

    def side_copies(q, lo, base, act):
        part = (pl.ds(0, q), pl.ds(lo, 2))
        both_ways("frames", f, (eo.at[(0,) + part], ed.at[(1,) + part]), (eo.at[(1,) + part], ed.at[(0,) + part]), es, er, base, act)

    sub = lax.broadcasted_iota(jnp.int32, (8, 128), 0)

    def edges(lo):
        def body(q, carry):
            for k in (lo, lo + 1):
                for s in range(2):
                    cols = slice(16 * s, 16 * s + 16)
                    at = 15 * s
                    own = pb[q, k, :, cols].astype(F32)[:, at, :]
                    above = tb[0, q, k, cols].astype(F32)[at:at + 1]
                    below = tb[1, q, k, cols].astype(F32)[at:at + 1]
                    outside = jnp.where(sub == 0, above, below)
                    eo[s, q, k] = jnp.concatenate([own, outside], axis=0).astype(BF)
            return carry
        return body

    def add_sums(table, per, kinds):
        def body(q, carry):
            for i, (_, at, nxt) in enumerate(kinds):
                a = slot_of(q, at)
                v = pb[a[0], a[1]].reshape(256, 128)
                if nxt is not None:
                    b = slot_of(q, nxt)
                    v = v + pb[b[0], b[1]].reshape(256, 128)
                v = v.astype(F32)
                scale = 1.0 if nxt is None else 0.5
                row = pl.ds(per * q + i, 1)
                table[0, row] = scale * jnp.sum(v, axis=0, keepdims=True)
                table[1, row] = scale * scale * jnp.sum(v * v, axis=0, keepdims=True)
            return carry
        lax.fori_loop(0, 8, body, 0)

    def reduce_rows(table, s1, r1, sem):
        half = table.shape[1] // 2
        s1[...] = gather_groups([table[k // 2, half * (k % 2):half * (k % 2) + half] for k in range(4)])
        copies = []
        for k in range(1, NR):
            cp = pltpu.make_async_remote_copy(
                src_ref=s1, dst_ref=r1.at[k - 1], send_sem=sem.at[0, k - 1], recv_sem=sem.at[1, k - 1],
                device_id={"rows": (r + k) % NR}, device_id_type=MESH)
            cp.start()
            copies.append(cp)
        return copies

    def reduce_frames(copies, s1, r1, s2, r2, sem):
        for cp in copies:
            cp.wait()
        total = s1[...]
        for k in range(NR - 1):
            total += r1[k]
        s2[...] = total
        copies = []
        for k in range(NF - 1):
            cp = pltpu.make_async_remote_copy(
                src_ref=s2, dst_ref=r2.at[k], send_sem=sem.at[0, k], recv_sem=sem.at[1, k],
                device_id={"frames": peer(f, k)}, device_id_type=MESH)
            cp.start()
            copies.append(cp)
        return copies

    def statistics(copies, s2, r2, out):
        for cp in copies:
            cp.wait()
        total = s2[...]
        for k in range(NF - 1):
            total += r2[k]
        count = 64 * 512 * 4
        half = out.shape[1] // 2
        for k in range(2):
            mean = spread_groups(total, k) / count
            square = spread_groups(total, k + 2) / count
            out[0, half * k:half * k + half] = mean
            out[1, half * k:half * k + half] = lax.rsqrt(square - mean * mean + 1e-05)

    for i in range(8):
        for dc in range(2):
            if i < 7 or dc:
                wait_in(pb.at[0, 2], ir.at[2 * i + dc])
    own_inner.wait()
    rows_copies(8, 2, 0, "start")
    add_sums(st_e, E_ROWS, EARLY)
    early_copies = reduce_rows(st_e, s1e, r1e, sem_e1)
    fill_weights(ws, w0, w1)
    blocks_not_end(2, 4)
    own_outer = pltpu.make_async_copy(so.at[3, c], pb.at[chip + c, pl.ds(0, 2)], lsem.at[1])
    own_outer.start()
    rows_copies(8, 2, 0, "wait")
    lax.fori_loop(0, 8, edges(2), 0)
    side_copies(8, 2, 0, "start")
    early_copies = reduce_frames(early_copies, s1e, r1e, s2e, r2e, sem_e2)

    for n in range(8):
        for dc in range(2):
            if n == 3 and dc == 0:
                continue
            if n < 4:
                wait_in(pb.at[0, pl.ds(0, 2)], or_.at[2 * n + dc])
            else:
                from_c = (c + dc) % 2
                sg = 2 * from_c - 1
                from_x = (x - (sg if n % 2 == 0 else 2 * sg) + 4) % 4
                from_dev = ((z + 1 - (n // 2) % 2) % 2) * 8 + from_x * 2 + from_c

                @pl.when((from_dev == 0) | (from_dev == NF - 1))
                def _():
                    wait_in(pb.at[0, pl.ds(0, 2)], or_.at[2 * n + dc])
    own_outer.wait()
    rows_copies(9, 0, 2, "start")
    add_sums(st_l, L_ROWS, LATE)
    late_copies = reduce_rows(st_l, s1l, r1l, sem_l1)
    pb_copy = pltpu.make_async_copy(pb, pb_out, osem.at[0])
    pb_copy.start()
    side_copies(8, 2, 0, "wait")
    nz_load.wait()
    statistics(early_copies, s2e, r2e, stat_e)

    keeps = border_keeps(f, r)

    def early_conv(q, carry):
        for i, (_, at, nxt) in enumerate(EARLY):
            norm_frame(slot_of(q, at), nxt and slot_of(q, nxt), E_ROWS * q + i, i,
                       pb, tb, ed, stat_e, gain, bias, ea.at[i], ll, None, keeps)
        rows = conv_rows(3, ll, w0, w1)
        for R in range(8):
            for i, (_, at, nxt) in enumerate(EARLY):
                v = pb[q, at[1], R]
                if nxt is not None:
                    v = v + pb[q, nxt[1], R]
                v = v.astype(F32) * (1.0 if nxt is None else 0.5)
                res_e[q, i, R] = (rows[R][i] + v + 0.3 * nz[q, i, R].astype(F32)).astype(BF)
        return carry

    lax.fori_loop(0, 4, early_conv, 0)
    late_copies = reduce_frames(late_copies, s1l, r1l, s2l, r2l, sem_l2)
    rows_copies(9, 0, 2, "wait")
    lax.fori_loop(0, 9, edges(0), 0)
    side_copies(9, 0, 2, "start")
    tb_copy = pltpu.make_async_copy(tb, tb_out, osem.at[1])
    tb_copy.start()
    lax.fori_loop(4, 8, early_conv, 0)
    early_copy = pltpu.make_async_copy(res_e, early_out, osem.at[3])
    early_copy.start()

    for i in range(8):
        inner_copy(i).wait_send()
        inner_send(i, 1).wait_send()
        if i < 7:
            inner_send(i, 0).wait_send()
    for n in range(4):
        outer_send(n, 1).wait_send()
        if n != 3:
            outer_send(n, 0).wait_send()

    @pl.when(not_end)
    def _():
        for n in range(2):
            halo_copy(n).wait_send()

    for n in range(2, 4):
        @pl.when(is_mid)
        def _():
            detour_copy(n).wait_send()

        @pl.when(jnp.logical_not(is_mid))
        def _():
            halo_copy(n).wait_send()

    @pl.when(is_end)
    def _():
        for n in range(4, 8):
            outer_send(n, 1).wait_send()
            outer_send(n, 0).wait_send()

    side_copies(9, 0, 2, "wait")
    ed_copy = pltpu.make_async_copy(ed, ed_out, osem.at[2])
    ed_copy.start()
    statistics(late_copies, s2l, r2l, st_out)
    pb_copy.wait()
    tb_copy.wait()
    ed_copy.wait()
    early_copy.wait()


def local(video, w_time, w_proj, w_space, gn_gain, gn_bias, noise):
    slots = 2 * NF + 4
    full = lambda shape: pl.BlockSpec(shape, lambda g: (0,) * len(shape))
    anyw = pl.BlockSpec(memory_space=pl.ANY)
    vm = pl.BlockSpec(memory_space=pltpu.VMEM)
    quads = slots // 4
    dma = pltpu.SemaphoreType.DMA
    gain, bias = gn_gain.reshape(1, 128), gn_bias.reshape(1, 128)
    pb, tb, ed, st, early = pl.pallas_call(
        move_kernel,
        out_shape=(
            jax.ShapeDtypeStruct((quads, 4, 8, 32, 128), BF),
            jax.ShapeDtypeStruct((2, quads, 4, 32, 128), BF),
            jax.ShapeDtypeStruct((2, quads, 4, 16, 128), BF),
            jax.ShapeDtypeStruct((2, 8 * L_ROWS, 128), F32),
            jax.ShapeDtypeStruct((8, 3, 8, 32, 128), BF),
        ),
        in_specs=[anyw, vm, vm, vm, vm, vm, anyw],
        out_specs=(anyw, anyw, anyw, vm, anyw),
        scratch_shapes=[
            pltpu.VMEM((2, 8, 512, 256), BF),
            pltpu.VMEM((8, 8, 64, 256), BF),
            pltpu.VMEM((4, 2, 8, 64, 256), BF),
            pltpu.VMEM((2, 2, 8, 64, 256), BF),
            pltpu.VMEM((768, 256), BF),
            pltpu.VMEM((8, 2, 8, 32, 128), BF),
            pltpu.VMEM((8, 2, 2, 8, 32, 128), BF),
            pltpu.VMEM((quads, 4, 8, 32, 128), BF),
            pltpu.VMEM((2, quads, 4, 32, 128), BF),
            pltpu.VMEM((2, quads, 4, 16, 128), BF),
            pltpu.VMEM((2, quads, 4, 16, 128), BF),
            pltpu.VMEM((2, 8 * E_ROWS, 128), F32),
            pltpu.VMEM((4 * E_ROWS, 128), F32),
            pltpu.VMEM((NR - 1, 4 * E_ROWS, 128), F32),
            pltpu.VMEM((4 * E_ROWS, 128), F32),
            pltpu.VMEM((NF - 1, 4 * E_ROWS, 128), F32),
            pltpu.VMEM((2, 8 * E_ROWS, 128), F32),
            pltpu.VMEM((2, 8 * L_ROWS, 128), F32),
            pltpu.VMEM((4 * L_ROWS, 128), F32),
            pltpu.VMEM((NR - 1, 4 * L_ROWS, 128), F32),
            pltpu.VMEM((4 * L_ROWS, 128), F32),
            pltpu.VMEM((NF - 1, 4 * L_ROWS, 128), F32),
            pltpu.VMEM((8, 3, 8, 32, 128), BF),
            pltpu.VMEM((768, 256), BF),
            pltpu.VMEM((768, 256), BF),
            pltpu.VMEM((5, 96, 768), BF),
            pltpu.VMEM((3, 2, 16, 128), F32),
            pltpu.VMEM((8, 3, 8, 32, 128), BF),
            dma((2,)),
            dma((8,)), dma((8,)),
            dma((4,)), dma((4,)),
            dma((2,)), dma((2,)),
            dma((16,)), dma((16,)),
            dma((16,)), dma((16,)),
            dma((4,)), dma((4,)),
            dma((4,)), dma((4,)),
            dma((2, NR - 1)), dma((2, NF - 1)),
            dma((2, NR - 1)), dma((2, NF - 1)),
            dma((5,)),
        ],
        compiler_params=pltpu.CompilerParams(collective_id=0, has_side_effects=True, vmem_limit_bytes=60 << 20),
        name="move",
    )(video, w_time, w_proj, w_space, gain, bias, noise.reshape(8, 8, 8, 32, 128))
    return pl.pallas_call(
        conv_kernel,
        grid=(9,),
        out_shape=jax.ShapeDtypeStruct((64, 8, 32, 128), BF),
        in_specs=[
            full((quads, 4, 8, 32, 128)), full((2, quads, 4, 32, 128)), full((2, quads, 4, 16, 128)), full((2, 8 * L_ROWS, 128)),
            pl.BlockSpec((1, 3, 8, 32, 128), lambda g: (jnp.maximum(g - 1, 0), 0, 0, 0, 0)),
            full((3, 3, 128, 128)), full((1, 128)), full((1, 128)),
            pl.BlockSpec((8, 8, 32, 128), lambda g: (jnp.maximum(g - 1, 0), 0, 0, 0)),
        ],
        out_specs=pl.BlockSpec((8, 8, 32, 128), lambda g: (jnp.maximum(g - 1, 0), 0, 0, 0)),
        scratch_shapes=[
            pltpu.VMEM((768, 256), BF),
            pltpu.VMEM((768, 256), BF),
            pltpu.VMEM((5, 160, 768), BF),
            pltpu.VMEM((5, 160, 768), BF),
            pltpu.VMEM((5, 8, 32, 128), BF),
            pltpu.VMEM((5, 8, 32, 128), BF),
            pltpu.VMEM((5, 2, 16, 128), F32),
        ],
        compiler_params=pltpu.CompilerParams(vmem_limit_bytes=60 << 20),
        name="conv",
    )(pb, tb, ed, st, early, w_space, gain, bias, noise)


def solution(mesh):
    in_specs = (
        P("frames", "rows", None, None),
        P(), P(), P(), P(), P(),
        P(None, "rows", "frames", None),
    )
    out_specs = P(None, "rows", "frames", None)
    return jax.shard_map(local, mesh=mesh, in_specs=in_specs, out_specs=out_specs, check_vma=False)
```

```python
import jax
import jax.numpy as jnp
from jax import lax
from jax.experimental import pallas as pl
from jax.experimental.pallas import tpu as pltpu
from jax.sharding import PartitionSpec as P

MESH = pl.DeviceIdType.MESH
NF, NR = 16, 8
GROUPS = 32
BF, F32 = jnp.bfloat16, jnp.float32

PEERS = [(dz, dx, dc) for dx in (2, 1, 3, 0) for dz in (1, 0) for dc in (0, 1) if (dz, dx, dc) != (0, 0, 0)]


def peer(f, k):
    dz, dx, dc = PEERS[k]
    z, x, c = f // 8, (f // 2) % 4, f % 2
    return ((z + dz) % 2) * 8 + ((x + dx) % 4) * 2 + (c + dc) % 2


def silu(v):
    h = 0.5 * v
    return h + h * jnp.tanh(h)


def gather_groups(parts):
    lane = lax.broadcasted_iota(jnp.int32, parts[0].shape, 1) & 3
    out = jnp.zeros(parts[0].shape, F32)
    for k, v in enumerate(parts):
        v = v + pltpu.roll(v, 127, 1)
        v = v + pltpu.roll(v, 126, 1)
        out = jnp.where(lane == k, pltpu.roll(v, k, 1) if k else v, out)
    return out


def spread_groups(v, k):
    lane = lax.broadcasted_iota(jnp.int32, v.shape, 1) & 3
    v = jnp.where(lane == k, v, 0.0)
    v = pltpu.roll(v, 128 - k, 1) if k else v
    v = v + pltpu.roll(v, 1, 1)
    return v + pltpu.roll(v, 2, 1)


def temporal(before, now, after, w3, wp):
    x = [v.reshape(512, 256) for v in (before, now, after)]
    taps = jnp.dot(jnp.concatenate(x, axis=1), w3[...], preferred_element_type=F32)
    mixed = (x[1].astype(F32) + silu(taps)).astype(BF)
    proj = jnp.dot(mixed, wp[...], preferred_element_type=F32).astype(BF)
    return proj.reshape(8, 2, 32, 128)


def border_keeps(f, r):
    return (jnp.where(r > 0, 1.0, 0.0), jnp.where(r < NR - 1, 1.0, 0.0),
            (jnp.where(f > 0, 1.0, 0.0), jnp.where(f < NF - 1, 1.0, 0.0)))


def norm_frame(now, nxt, line, place, pb, tb, ed, st, gain, bias, ea, ll, fld, keeps):
    keep_top, keep_bottom, keep_side = keeps
    line = pl.ds(line, 1)
    scale = st[1, line] * gain[...]
    shift = 0.5 * (bias[...] - st[0, line] * scale)
    scale = (0.5 if nxt is None else 0.25) * scale
    sub = lax.broadcasted_iota(jnp.int32, (8, 128), 0)

    def act_of(ref, before, after, keep=None):
        v = ref[before + now + after]
        if nxt is not None:
            v = v + ref[before + nxt + after]
        if keep is not None:
            keep[...] = v
        h = v.astype(F32) * scale + shift
        return h + h * jnp.tanh(h)

    for s in range(2):
        ea[s] = act_of(ed, (s,), ()) * keep_side[s]
    for R in range(10):
        E = 8 if R == 0 else R - 1 if R < 9 else 9
        el, er = ea[0, E:E + 1], ea[1, E:E + 1]
        if R == 0:
            a = act_of(tb, (0,), ()) * keep_top
            el, er = el * keep_top, er * keep_top
        elif R == 9:
            a = act_of(tb, (1,), ()) * keep_bottom
            el, er = el * keep_bottom, er * keep_bottom
        else:
            a = act_of(pb, (), (R - 1,), None if fld is None else fld.at[place, R - 1])
        tiles = [a[8 * i:8 * i + 8] for i in range(4)]
        down = [pltpu.roll(v, 1, 0) for v in tiles]
        up = [pltpu.roll(v, 7, 0) for v in tiles]
        left = [jnp.where(sub == 0, down[i - 1] if i else el, down[i]) for i in range(4)]
        right = [jnp.where(sub == 7, up[i + 1] if i < 3 else er, up[i]) for i in range(4)]
        for j, v in enumerate((jnp.concatenate(left, 0), a, jnp.concatenate(right, 0))):
            lane = 256 * j + 128 * (R % 2)
            ll[R // 2, 32 * place:32 * place + 32, lane:lane + 128] = v.astype(BF)


def fill_weights(ws, w0, w1):
    zero = jnp.zeros((128, 128), BF)
    for j in range(3):
        for a in range(2):
            for b in range(2):
                i = a - b
                at = (slice(256 * j + 128 * a, 256 * j + 128 * a + 128), slice(128 * b, 128 * b + 128))
                w0[at] = ws[i, j] if 0 <= i else zero
                i = 2 + a - b
                w1[at] = ws[i, j] if i <= 2 else zero


def conv_rows(count, ll, w0, w1):
    m = 32 * count
    sides = jnp.concatenate([ll[0:4].reshape(4 * m, 768), ll[1:5].reshape(4 * m, 768)], axis=1)
    res = jnp.dot(sides, jnp.concatenate([w0[...], w1[...]], axis=0), preferred_element_type=F32)
    return [res[m * (R // 2):m * (R // 2) + m, 128 * (R % 2):128 * (R % 2) + 128].reshape(count, 32, 128)
            for R in range(8)]


def conv_kernel(
    pb_in, tb_in, ed_in, st, early, ws_in, gain, bias, noise, out,
    pb, tb, ed, ws, nz, res, w0, w1, ll_a, ll_b, fld_a, fld_b, ea, qsem, nsem, osem, wsem,
):
    f, r = lax.axis_index("frames"), lax.axis_index("rows")
    keeps = border_keeps(f, r)
    steps = noise.shape[0]

    def quad_loads(k):
        lo, n = ((0, 2), (2, 2), (4, 5))[k]
        at = pl.ds(lo, n)
        return [pltpu.make_async_copy(pb_in.at[at], pb.at[at], qsem.at[k, 0]),
                pltpu.make_async_copy(tb_in.at[:, at], tb.at[:, at], qsem.at[k, 1]),
                pltpu.make_async_copy(ed_in.at[:, at], ed.at[:, at], qsem.at[k, 2])]

    def frame_loads(k):
        lo, n = ((0, 2), (2, 6))[k]
        at = pl.ds(lo, n)
        return [pltpu.make_async_copy(noise.at[at, pl.ds(0, 2)], nz.at[at, pl.ds(0, 2)], nsem.at[k, 0]),
                pltpu.make_async_copy(noise.at[at, pl.ds(5, 3)], nz.at[at, pl.ds(2, 3)], nsem.at[k, 1]),
                pltpu.make_async_copy(early.at[at], res.at[at, pl.ds(2, 3)], nsem.at[k, 2])]

    def store(q):
        return pltpu.make_async_copy(res.at[q], out.at[q], osem.at[q])

    weights = pltpu.make_async_copy(ws_in, ws, wsem)
    for cp in quad_loads(0) + [weights]:
        cp.start()

    def step(g, new, old):
        if new is not None:
            ll, fld = new
            for i, (_, at, nxt) in enumerate(LATE):
                norm_frame(slot_of(g, at), nxt and slot_of(g, nxt), L_ROWS * g + i, i,
                           pb, tb, ed, st, gain, bias, ea.at[i], ll, fld, keeps)
        if old is not None:
            h = g - 1
            ll, fld = old
            rows = conv_rows(len(LATE), ll, w0, w1)
            for R in range(8):
                for i, (k, _, nxt) in enumerate(LATE):
                    v = fld[i, R].astype(F32) * (1.0 if nxt is None else 0.5)
                    res[h, k, R] = (rows[R][i] + v + 0.3 * nz[h, i, R].astype(F32)).astype(BF)

    a, b = (ll_a, fld_a), (ll_b, fld_b)
    for cp in quad_loads(0):
        cp.wait()
    for cp in quad_loads(1) + frame_loads(0):
        cp.start()
    step(0, a, None)
    weights.wait()
    fill_weights(ws, w0, w1)

    def pair(i, carry):
        for k in range(2):
            @pl.when(i == k)
            def _():
                for cp in quad_loads(k + 1) + frame_loads(k):
                    cp.wait()
                if k == 0:
                    for cp in quad_loads(2) + frame_loads(1):
                        cp.start()

        @pl.when(i > 0)
        def _():
            for k in range(2):
                store(2 * i - 2 + k).start()

        step(2 * i + 1, b, a)
        step(2 * i + 2, a, b)
        return carry

    lax.fori_loop(0, steps // 2 - 1, pair, 0)
    for q in range(steps - 4, steps - 2):
        store(q).start()
    step(steps - 1, b, a)
    store(steps - 2).start()
    step(steps, None, b)
    store(steps - 1).start()
    for q in range(steps):
        store(q).wait()


EARLY = ((2, (0, 2), None), (3, (0, 2), (0, 3)), (4, (0, 3), None))
LATE = ((0, (0, 1), None), (1, (0, 1), (0, 2)), (5, (0, 3), (1, 0)), (6, (1, 0), None), (7, (1, 0), (1, 1)))
HALO_AT = ((0,), (1, 2, 3))
E_ROWS, L_ROWS = 4, 6


def slot_of(q, at):
    if at == (1, 1):
        return q + 1, jnp.where(q == 7, 0, 1)
    return q + at[0], at[1]


def move_kernel(
    video, wt_in, wp_in, ws_in, gain_in, bias_in, noise, pb_out, tb_out, ed_out, st_out, early_out,
    wt, wp, ws, gain, bias, vv, inner, halo, relay, w3, si, so, pb, tb, eo, ed,
    st_e, s1e, r1e, s2e, r2e, stat_e, st_l, s1l, r1l, s2l, r2l,
    nz, w0, w1, ll, ea, res_e,
    lsem, ns, nr, hs, hr, ls, lr, is_, ir, os, or_, ts, tr, es, er, sem_e1, sem_e2, sem_l1, sem_l2, osem, wsem,
):
    f, r = lax.axis_index("frames"), lax.axis_index("rows")
    z, x, c = f // 8, (f // 2) % 4, f % 2
    chip = f // 2
    sgn = 2 * c - 1
    is_end = (f == 0) | (f == NF - 1)
    not_end = jnp.logical_not(is_end)
    outer_frame, inner_frame = c, 1 - c
    outer_dev = jnp.clip(f + sgn, 0, NF - 1)
    inner_dev = f + 1 - 2 * c

    def wait_in(ref, sem):
        pltpu.make_async_copy(ref, ref, sem).wait()

    def column(zz, xx):
        return pl.ds(pl.multiple_of(zz * 256 + xx * 64, 64), 64)

    def far_first(i):
        j = i // 2
        dx = jnp.where(j == 0, 2, jnp.where(j == 1, 1, jnp.where(j == 2, 3, 0)))
        return (z + 1 - i % 2) % 2, (x + dx) % 4

    def near_first(n, zz, xx, sg):
        dx = jnp.where(n < 4, jnp.where(n % 2 == 0, -sg, 0), jnp.where(n % 2 == 0, sg, 2 * sg))
        return (zz + 1 - (n // 2) % 2) % 2, (xx + dx + 4) % 4

    barrier = pltpu.get_barrier_semaphore()
    for k in range(NF - 1):
        pl.semaphore_signal(barrier, inc=1, device_id={"frames": peer(f, k)}, device_id_type=MESH)
    for k in range(1, NR):
        pl.semaphore_signal(barrier, inc=1, device_id={"rows": (r + k) % NR}, device_id_type=MESH)
    nz_load = pltpu.make_async_copy(noise.at[:, pl.ds(2, 3)], nz, osem.at[4])
    nz_load.start()
    loads = [pltpu.make_async_copy(video.at[k], vv.at[k], lsem.at[k]) for k in range(2)]
    for cp in loads:
        cp.start()
    small = [pltpu.make_async_copy(a, b, wsem.at[k]) for k, (a, b) in enumerate(
        ((wt_in, wt), (wp_in, wp), (ws_in, ws), (gain_in, gain), (bias_in, bias)))]
    for cp in small:
        cp.start()
    for cp in small[:2]:
        cp.wait()
    w3[0:256] = wt[2 - 2 * c]
    w3[256:512] = wt[1]
    w3[512:768] = wt[2 * c]

    @pl.when(is_end)
    def _():
        halo[...] = jnp.zeros(halo.shape, BF)

    for axis_at, ref in ((r, tb), (f, ed)):
        count = NR if ref is tb else NF
        for side, edge in ((0, 0), (1, count - 1)):
            @pl.when(axis_at == edge)
            def _():
                ref[side] = jnp.zeros(ref.shape[1:], BF)

    pb[0, 0] = jnp.zeros(pb.shape[2:], BF)
    pb[8, 1] = jnp.zeros(pb.shape[2:], BF)
    st_e[...] = jnp.zeros(st_e.shape, F32)
    st_l[...] = jnp.zeros(st_l.shape, F32)
    pl.semaphore_wait(barrier, NF + NR - 2)

    is_mid = (f == NF // 2 - 1) | (f == NF // 2)

    def halo_copy(n):
        zz, xx = near_first(n, outer_dev // 8, (x + sgn + 4) % 4, -sgn)
        return pltpu.make_async_remote_copy(
            src_ref=video.at[:, :, column(zz, xx)], dst_ref=halo.at[n], send_sem=hs.at[n], recv_sem=hr.at[n],
            device_id={"frames": outer_dev}, device_id_type=MESH)

    def detour_copy(n):
        zz, xx = near_first(n, outer_dev // 8, (x + sgn + 4) % 4, -sgn)
        return pltpu.make_async_remote_copy(
            src_ref=video.at[:, :, column(zz, xx)], dst_ref=relay.at[n - 2], send_sem=ls.at[n - 2], recv_sem=lr.at[n - 2],
            device_id={"frames": jnp.where(f < NF // 2, NF - 1, 0)}, device_id_type=MESH)

    def relay_copy(n):
        return pltpu.make_async_remote_copy(
            src_ref=relay.at[n - 2], dst_ref=halo.at[n], send_sem=hs.at[n], recv_sem=hr.at[n],
            device_id={"frames": jnp.where(f < NF // 2, NF // 2 - 1, NF // 2)}, device_id_type=MESH)

    def inner_copy(i):
        zz, xx = far_first(i)
        return pltpu.make_async_remote_copy(
            src_ref=video.at[inner_frame, :, column(zz, xx)], dst_ref=inner.at[i], send_sem=ns.at[i], recv_sem=nr.at[i],
            device_id={"frames": inner_dev}, device_id_type=MESH)

    for i in range(8):
        inner_copy(i).start()

    def halo_start(blocks):
        for n in blocks:
            if n < 2:
                @pl.when(not_end)
                def _():
                    halo_copy(n).start()
            else:
                @pl.when(not_end & jnp.logical_not(is_mid))
                def _():
                    halo_copy(n).start()

    @pl.when(is_mid)
    def _():
        for n in (2, 3):
            detour_copy(n).start()

    halo_start(HALO_AT[0])

    for cp in loads:
        cp.wait()

    def inner_send(i, dc):
        zz, xx = far_first(i)
        dest = zz * 8 + xx * 2 + (c + dc) % 2
        slot = 2 * i + dc
        return pltpu.make_async_remote_copy(
            src_ref=si.at[i, (c + dc) % 2], dst_ref=pb.at[chip, 2 + c], send_sem=is_.at[slot], recv_sem=ir.at[slot],
            device_id={"frames": dest}, device_id_type=MESH)

    def inner_block(i, carry):
        zz, xx = far_first(i)
        wait_in(inner.at[i], nr.at[i])
        here = column(zz, xx)
        proj = temporal(inner[i], vv[inner_frame, :, here], vv[outer_frame, :, here], w3, wp)
        for h in range(2):
            si[i, h] = proj[:, h]
        inner_send(i, 1).start()

        @pl.when(i < 7)
        def _():
            inner_send(i, 0).start()

        return carry

    lax.fori_loop(0, 8, inner_block, 0)
    own_inner = pltpu.make_async_copy(si.at[7, c], pb.at[chip, 2 + c], lsem.at[0])
    own_inner.start()

    def outer_send(n, dc, alone):
        zz, xx = near_first(n, z, x, sgn)
        dest = zz * 8 + xx * 2 + (c + dc) % 2
        slot = 2 * n + dc
        src, dst = so.at[n, (c + dc) % 2], pb.at[chip + c]
        at = 1 - c if alone else pl.ds(0, 2)
        return pltpu.make_async_remote_copy(
            src_ref=src.at[at], dst_ref=dst.at[at], send_sem=os.at[slot], recv_sem=or_.at[slot],
            device_id={"frames": dest}, device_id_type=MESH)

    def outer_part(n, dc, act):
        @pl.when(is_end)
        def _():
            cp = outer_send(n, dc, True)
            cp.start() if act == "start" else cp.wait_send()

        if not (isinstance(n, int) and n > 3):
            @pl.when(not_end)
            def _():
                cp = outer_send(n, dc, False)
                cp.start() if act == "start" else cp.wait_send()

    def outer_block(n, carry):
        zz, xx = near_first(n, z, x, sgn)
        here = column(zz, xx)
        at = n % 4

        @pl.when(not_end)
        def _():
            wait_in(halo.at[at], hr.at[at])

        proj = temporal(vv[inner_frame, :, here], vv[outer_frame, :, here], halo[at, 1 - c], w3, wp)
        for h in range(2):
            so[n, h, 1 - c] = proj[:, h]

        @pl.when(not_end)
        def _():
            proj = temporal(vv[outer_frame, :, here], halo[at, 1 - c], halo[at, c], w3, wp)
            for h in range(2):
                so[n, h, c] = proj[:, h]

        outer_part(n, 1, "start")

        @pl.when(n != 3)
        def _():
            outer_part(n, 0, "start")

        return carry

    def outer_blocks(first, past):
        lax.fori_loop(first, past, outer_block, 0)

    halo_start(HALO_AT[1])

    @pl.when(is_end)
    def _():
        outer_blocks(4, 8)
        outer_blocks(0, 4)
        for n in (2, 3):
            wait_in(relay.at[n - 2], lr.at[n - 2])
            relay_copy(n).start()

    def blocks_not_end(first, past):
        @pl.when(not_end)
        def _():
            outer_blocks(first, past)

    blocks_not_end(0, 2)

    def both_ways(axis, at, up_refs, down_refs, ssem, rsem, base, act):
        count = lax.axis_size(axis)
        first, last = at == 0, at == count - 1
        up = pltpu.make_async_remote_copy(
            src_ref=up_refs[0], dst_ref=up_refs[1], send_sem=ssem.at[base], recv_sem=rsem.at[base],
            device_id={axis: jnp.maximum(at - 1, 0)}, device_id_type=MESH)
        down = pltpu.make_async_remote_copy(
            src_ref=down_refs[0], dst_ref=down_refs[1], send_sem=ssem.at[base + 1], recv_sem=rsem.at[base + 1],
            device_id={axis: jnp.minimum(at + 1, count - 1)}, device_id_type=MESH)

        @pl.when(jnp.logical_not(first))
        def _():
            if act == "start":
                up.start()
            else:
                up.wait_send()
                down.wait_recv()

        @pl.when(jnp.logical_not(last))
        def _():
            if act == "start":
                down.start()
            else:
                down.wait_send()
                up.wait_recv()

    def rows_copies(q, lo, base, act):
        part = (pl.ds(0, q), pl.ds(lo, 2))
        both_ways("rows", r, (pb.at[part + (0,)], tb.at[(1,) + part]), (pb.at[part + (7,)], tb.at[(0,) + part]), ts, tr, base, act)

    def side_copies(q, lo, base, act):
        part = (pl.ds(0, q), pl.ds(lo, 2))
        both_ways("frames", f, (eo.at[(0,) + part], ed.at[(1,) + part]), (eo.at[(1,) + part], ed.at[(0,) + part]), es, er, base, act)

    sub = lax.broadcasted_iota(jnp.int32, (8, 128), 0)

    def edges(lo):
        def body(q, carry):
            for k in (lo, lo + 1):
                for s in range(2):
                    cols = slice(16 * s, 16 * s + 16)
                    at = 15 * s
                    own = pb[q, k, :, cols].astype(F32)[:, at, :]
                    above = tb[0, q, k, cols].astype(F32)[at:at + 1]
                    below = tb[1, q, k, cols].astype(F32)[at:at + 1]
                    outside = jnp.where(sub == 0, above, below)
                    eo[s, q, k] = jnp.concatenate([own, outside], axis=0).astype(BF)
            return carry
        return body

    def add_sums(table, per, kinds):
        def body(q, carry):
            for i, (_, at, nxt) in enumerate(kinds):
                a = slot_of(q, at)
                v = pb[a[0], a[1]].reshape(256, 128)
                if nxt is not None:
                    b = slot_of(q, nxt)
                    v = v + pb[b[0], b[1]].reshape(256, 128)
                v = v.astype(F32)
                scale = 1.0 if nxt is None else 0.5
                row = pl.ds(per * q + i, 1)
                table[0, row] = scale * jnp.sum(v, axis=0, keepdims=True)
                table[1, row] = scale * scale * jnp.sum(v * v, axis=0, keepdims=True)
            return carry
        lax.fori_loop(0, 8, body, 0)

    def reduce_rows(table, s1, r1, sem):
        half = table.shape[1] // 2
        s1[...] = gather_groups([table[k // 2, half * (k % 2):half * (k % 2) + half] for k in range(4)])
        copies = []
        for k in range(1, NR):
            cp = pltpu.make_async_remote_copy(
                src_ref=s1, dst_ref=r1.at[k - 1], send_sem=sem.at[0, k - 1], recv_sem=sem.at[1, k - 1],
                device_id={"rows": (r + k) % NR}, device_id_type=MESH)
            cp.start()
            copies.append(cp)
        return copies

    def reduce_frames(copies, s1, r1, s2, r2, sem):
        for cp in copies:
            cp.wait()
        total = s1[...]
        for k in range(NR - 1):
            total += r1[k]
        s2[...] = total
        copies = []
        for k in range(NF - 1):
            cp = pltpu.make_async_remote_copy(
                src_ref=s2, dst_ref=r2.at[k], send_sem=sem.at[0, k], recv_sem=sem.at[1, k],
                device_id={"frames": peer(f, k)}, device_id_type=MESH)
            cp.start()
            copies.append(cp)
        return copies

    def statistics(copies, s2, r2, out):
        for cp in copies:
            cp.wait()
        total = s2[...]
        for k in range(NF - 1):
            total += r2[k]
        count = 64 * 512 * 4
        half = out.shape[1] // 2
        for k in range(2):
            mean = spread_groups(total, k) / count
            square = spread_groups(total, k + 2) / count
            out[0, half * k:half * k + half] = mean
            out[1, half * k:half * k + half] = lax.rsqrt(square - mean * mean + 1e-05)

    for i in range(8):
        for dc in range(2):
            if i < 7 or dc:
                wait_in(pb.at[0, 2], ir.at[2 * i + dc])
    own_inner.wait()
    rows_copies(8, 2, 0, "start")
    add_sums(st_e, E_ROWS, EARLY)
    early_copies = reduce_rows(st_e, s1e, r1e, sem_e1)
    for cp in small[2:]:
        cp.wait()
    fill_weights(ws, w0, w1)
    blocks_not_end(2, 3)
    rows_copies(8, 2, 0, "wait")
    lax.fori_loop(0, 8, edges(2), 0)
    side_copies(8, 2, 0, "start")
    early_copies = reduce_frames(early_copies, s1e, r1e, s2e, r2e, sem_e2)
    blocks_not_end(3, 4)
    own_pair = pltpu.make_async_copy(so.at[3, c], pb.at[chip + c, pl.ds(0, 2)], lsem.at[1])
    own_frame = pltpu.make_async_copy(so.at[3, c, 1 - c], pb.at[chip + c, 1 - c], lsem.at[1])

    @pl.when(not_end)
    def _():
        own_pair.start()

    @pl.when(is_end)
    def _():
        own_frame.start()


    for n in range(8):
        for dc in range(2):
            if n == 3 and dc == 0:
                continue
            from_c = (c + dc) % 2
            sg = 2 * from_c - 1
            dx = (sg * (1 + n % 2)) if n > 3 else -sg if n % 2 == 0 else 0
            from_dev = ((z + 1 - (n // 2) % 2) % 2) * 8 + ((x - dx + 4) % 4) * 2 + from_c
            from_end = (from_dev == 0) | (from_dev == NF - 1)

            @pl.when(from_end)
            def _():
                wait_in(pb.at[0, 0], or_.at[2 * n + dc])

            if n < 4:
                @pl.when(jnp.logical_not(from_end))
                def _():
                    wait_in(pb.at[0, pl.ds(0, 2)], or_.at[2 * n + dc])

    @pl.when(not_end)
    def _():
        own_pair.wait()

    @pl.when(is_end)
    def _():
        own_frame.wait()

    rows_copies(9, 0, 2, "start")
    add_sums(st_l, L_ROWS, LATE)
    late_copies = reduce_rows(st_l, s1l, r1l, sem_l1)
    pb_copy = pltpu.make_async_copy(pb, pb_out, osem.at[0])
    pb_copy.start()
    side_copies(8, 2, 0, "wait")
    nz_load.wait()
    statistics(early_copies, s2e, r2e, stat_e)

    keeps = border_keeps(f, r)

    def early_conv(q, carry):
        for i, (_, at, nxt) in enumerate(EARLY):
            norm_frame(slot_of(q, at), nxt and slot_of(q, nxt), E_ROWS * q + i, i,
                       pb, tb, ed, stat_e, gain, bias, ea.at[i], ll, None, keeps)
        rows = conv_rows(3, ll, w0, w1)
        for R in range(8):
            for i, (_, at, nxt) in enumerate(EARLY):
                v = pb[q, at[1], R]
                if nxt is not None:
                    v = v + pb[q, nxt[1], R]
                v = v.astype(F32) * (1.0 if nxt is None else 0.5)
                res_e[q, i, R] = (rows[R][i] + v + 0.3 * nz[q, i, R].astype(F32)).astype(BF)
        return carry

    lax.fori_loop(0, 4, early_conv, 0)
    late_copies = reduce_frames(late_copies, s1l, r1l, s2l, r2l, sem_l2)
    rows_copies(9, 0, 2, "wait")
    lax.fori_loop(0, 9, edges(0), 0)
    side_copies(9, 0, 2, "start")
    tb_copy = pltpu.make_async_copy(tb, tb_out, osem.at[1])
    tb_copy.start()
    lax.fori_loop(4, 8, early_conv, 0)
    early_copy = pltpu.make_async_copy(res_e, early_out, osem.at[3])
    early_copy.start()

    for i in range(8):
        inner_copy(i).wait_send()
        inner_send(i, 1).wait_send()
        if i < 7:
            inner_send(i, 0).wait_send()
    for n in range(4):
        outer_part(n, 1, "wait")
        if n != 3:
            outer_part(n, 0, "wait")

    @pl.when(not_end)
    def _():
        for n in range(2):
            halo_copy(n).wait_send()

    for n in range(2, 4):
        @pl.when(is_mid)
        def _():
            detour_copy(n).wait_send()

        @pl.when(jnp.logical_not(is_mid))
        def _():
            halo_copy(n).wait_send()

    @pl.when(is_end)
    def _():
        for n in range(4, 8):
            outer_send(n, 1, True).wait_send()
            outer_send(n, 0, True).wait_send()

    side_copies(9, 0, 2, "wait")
    ed_copy = pltpu.make_async_copy(ed, ed_out, osem.at[2])
    ed_copy.start()
    statistics(late_copies, s2l, r2l, st_out)
    pb_copy.wait()
    tb_copy.wait()
    ed_copy.wait()
    early_copy.wait()


def local(video, w_time, w_proj, w_space, gn_gain, gn_bias, noise):
    slots = 2 * NF + 4
    anyw = pl.BlockSpec(memory_space=pl.ANY)
    vm = pl.BlockSpec(memory_space=pltpu.VMEM)
    quads = slots // 4
    dma = pltpu.SemaphoreType.DMA
    gain, bias = gn_gain.reshape(1, 128), gn_bias.reshape(1, 128)
    noise = noise.reshape(8, 8, 8, 32, 128)
    pb, tb, ed, st, early = pl.pallas_call(
        move_kernel,
        out_shape=(
            jax.ShapeDtypeStruct((quads, 4, 8, 32, 128), BF),
            jax.ShapeDtypeStruct((2, quads, 4, 32, 128), BF),
            jax.ShapeDtypeStruct((2, quads, 4, 16, 128), BF),
            jax.ShapeDtypeStruct((2, 8 * L_ROWS, 128), F32),
            jax.ShapeDtypeStruct((8, 3, 8, 32, 128), BF),
        ),
        in_specs=[anyw, anyw, anyw, anyw, anyw, anyw, anyw],
        out_specs=(anyw, anyw, anyw, vm, anyw),
        scratch_shapes=[
            pltpu.VMEM((3, 256, 256), BF),
            pltpu.VMEM((256, 128), BF),
            pltpu.VMEM((3, 3, 128, 128), BF),
            pltpu.VMEM((1, 128), F32),
            pltpu.VMEM((1, 128), F32),
            pltpu.VMEM((2, 8, 512, 256), BF),
            pltpu.VMEM((8, 8, 64, 256), BF),
            pltpu.VMEM((4, 2, 8, 64, 256), BF),
            pltpu.VMEM((2, 2, 8, 64, 256), BF),
            pltpu.VMEM((768, 256), BF),
            pltpu.VMEM((8, 2, 8, 32, 128), BF),
            pltpu.VMEM((8, 2, 2, 8, 32, 128), BF),
            pltpu.VMEM((quads, 4, 8, 32, 128), BF),
            pltpu.VMEM((2, quads, 4, 32, 128), BF),
            pltpu.VMEM((2, quads, 4, 16, 128), BF),
            pltpu.VMEM((2, quads, 4, 16, 128), BF),
            pltpu.VMEM((2, 8 * E_ROWS, 128), F32),
            pltpu.VMEM((4 * E_ROWS, 128), F32),
            pltpu.VMEM((NR - 1, 4 * E_ROWS, 128), F32),
            pltpu.VMEM((4 * E_ROWS, 128), F32),
            pltpu.VMEM((NF - 1, 4 * E_ROWS, 128), F32),
            pltpu.VMEM((2, 8 * E_ROWS, 128), F32),
            pltpu.VMEM((2, 8 * L_ROWS, 128), F32),
            pltpu.VMEM((4 * L_ROWS, 128), F32),
            pltpu.VMEM((NR - 1, 4 * L_ROWS, 128), F32),
            pltpu.VMEM((4 * L_ROWS, 128), F32),
            pltpu.VMEM((NF - 1, 4 * L_ROWS, 128), F32),
            pltpu.VMEM((8, 3, 8, 32, 128), BF),
            pltpu.VMEM((768, 256), BF),
            pltpu.VMEM((768, 256), BF),
            pltpu.VMEM((5, 96, 768), BF),
            pltpu.VMEM((3, 2, 16, 128), F32),
            pltpu.VMEM((8, 3, 8, 32, 128), BF),
            dma((2,)),
            dma((8,)), dma((8,)),
            dma((4,)), dma((4,)),
            dma((2,)), dma((2,)),
            dma((16,)), dma((16,)),
            dma((16,)), dma((16,)),
            dma((4,)), dma((4,)),
            dma((4,)), dma((4,)),
            dma((2, NR - 1)), dma((2, NF - 1)),
            dma((2, NR - 1)), dma((2, NF - 1)),
            dma((5,)),
            dma((5,)),
        ],
        compiler_params=pltpu.CompilerParams(collective_id=0, has_side_effects=True, vmem_limit_bytes=60 << 20),
        name="move",
    )(video, w_time, w_proj, w_space, gain, bias, noise)
    out = pl.pallas_call(
        conv_kernel,
        out_shape=jax.ShapeDtypeStruct((8, 8, 8, 32, 128), BF),
        in_specs=[anyw, anyw, anyw, vm, anyw, anyw, vm, vm, anyw],
        out_specs=anyw,
        scratch_shapes=[
            pltpu.VMEM((quads, 4, 8, 32, 128), BF),
            pltpu.VMEM((2, quads, 4, 32, 128), BF),
            pltpu.VMEM((2, quads, 4, 16, 128), BF),
            pltpu.VMEM((3, 3, 128, 128), BF),
            pltpu.VMEM((8, 5, 8, 32, 128), BF),
            pltpu.VMEM((8, 8, 8, 32, 128), BF),
            pltpu.VMEM((768, 256), BF),
            pltpu.VMEM((768, 256), BF),
            pltpu.VMEM((5, 160, 768), BF),
            pltpu.VMEM((5, 160, 768), BF),
            pltpu.VMEM((5, 8, 32, 128), BF),
            pltpu.VMEM((5, 8, 32, 128), BF),
            pltpu.VMEM((5, 2, 16, 128), F32),
            dma((3, 3)), dma((2, 3)), dma((8,)), dma,
        ],
        compiler_params=pltpu.CompilerParams(vmem_limit_bytes=60 << 20),
        name="conv",
    )(pb, tb, ed, st, early, w_space, gain, bias, noise)
    return out.reshape(64, 8, 32, 128)


def solution(mesh):
    in_specs = (
        P("frames", "rows", None, None),
        P(), P(), P(), P(), P(),
        P(None, "rows", "frames", None),
    )
    out_specs = P(None, "rows", "frames", None)
    return jax.shard_map(local, mesh=mesh, in_specs=in_specs, out_specs=out_specs, check_vma=False)
```

```python
import jax
import jax.numpy as jnp
from jax import lax
from jax.experimental import pallas as pl
from jax.experimental.pallas import tpu as pltpu
from jax.sharding import PartitionSpec as P

MESH = pl.DeviceIdType.MESH
NF, NR = 16, 8
GROUPS = 32
BF, F32 = jnp.bfloat16, jnp.float32

PEERS = [(dz, dx, dc) for dx in (2, 1, 3, 0) for dz in (1, 0) for dc in (0, 1) if (dz, dx, dc) != (0, 0, 0)]


def peer(f, k):
    dz, dx, dc = PEERS[k]
    z, x, c = f // 8, (f // 2) % 4, f % 2
    return ((z + dz) % 2) * 8 + ((x + dx) % 4) * 2 + (c + dc) % 2


def silu(v):
    h = 0.5 * v
    return h + h * jnp.tanh(h)


def gather_groups(parts):
    lane = lax.broadcasted_iota(jnp.int32, parts[0].shape, 1) & 3
    out = jnp.zeros(parts[0].shape, F32)
    for k, v in enumerate(parts):
        v = v + pltpu.roll(v, 127, 1)
        v = v + pltpu.roll(v, 126, 1)
        out = jnp.where(lane == k, pltpu.roll(v, k, 1) if k else v, out)
    return out


def spread_groups(v, k):
    lane = lax.broadcasted_iota(jnp.int32, v.shape, 1) & 3
    v = jnp.where(lane == k, v, 0.0)
    v = pltpu.roll(v, 128 - k, 1) if k else v
    v = v + pltpu.roll(v, 1, 1)
    return v + pltpu.roll(v, 2, 1)


def temporal(before, now, after, w3, wp):
    x = [v.reshape(512, 256) for v in (before, now, after)]
    taps = jnp.dot(jnp.concatenate(x, axis=1), w3[...], preferred_element_type=F32)
    mixed = (x[1].astype(F32) + silu(taps)).astype(BF)
    proj = jnp.dot(mixed, wp[...], preferred_element_type=F32).astype(BF)
    return proj.reshape(8, 2, 32, 128)


def border_keeps(f, r):
    return (jnp.where(r > 0, 1.0, 0.0), jnp.where(r < NR - 1, 1.0, 0.0),
            (jnp.where(f > 0, 1.0, 0.0), jnp.where(f < NF - 1, 1.0, 0.0)))


def norm_frame(now, nxt, line, place, pb, tb, ed, st, gain, bias, ea, ll, fld, keeps):
    keep_top, keep_bottom, keep_side = keeps
    line = pl.ds(line, 1)
    scale = st[1, line] * gain[...]
    shift = 0.5 * (bias[...] - st[0, line] * scale)
    scale = (0.5 if nxt is None else 0.25) * scale
    sub = lax.broadcasted_iota(jnp.int32, (8, 128), 0)

    def act_of(ref, before, after, keep=None):
        v = ref[before + now + after]
        if nxt is not None:
            v = v + ref[before + nxt + after]
        if keep is not None:
            keep[...] = v
        h = v.astype(F32) * scale + shift
        return h + h * jnp.tanh(h)

    for s in range(2):
        ea[s] = act_of(ed, (s,), ()) * keep_side[s]
    for R in range(10):
        E = 8 if R == 0 else R - 1 if R < 9 else 9
        el, er = ea[0, E:E + 1], ea[1, E:E + 1]
        if R == 0:
            a = act_of(tb, (0,), ()) * keep_top
            el, er = el * keep_top, er * keep_top
        elif R == 9:
            a = act_of(tb, (1,), ()) * keep_bottom
            el, er = el * keep_bottom, er * keep_bottom
        else:
            a = act_of(pb, (), (R - 1,), None if fld is None else fld.at[place, R - 1])
        tiles = [a[8 * i:8 * i + 8] for i in range(4)]
        down = [pltpu.roll(v, 1, 0) for v in tiles]
        up = [pltpu.roll(v, 7, 0) for v in tiles]
        left = [jnp.where(sub == 0, down[i - 1] if i else el, down[i]) for i in range(4)]
        right = [jnp.where(sub == 7, up[i + 1] if i < 3 else er, up[i]) for i in range(4)]
        for j, v in enumerate((jnp.concatenate(left, 0), a, jnp.concatenate(right, 0))):
            lane = 256 * j + 128 * (R % 2)
            ll[R // 2, 32 * place:32 * place + 32, lane:lane + 128] = v.astype(BF)


def fill_weights(ws, w0, w1):
    zero = jnp.zeros((128, 128), BF)
    for j in range(3):
        for a in range(2):
            for b in range(2):
                i = a - b
                at = (slice(256 * j + 128 * a, 256 * j + 128 * a + 128), slice(128 * b, 128 * b + 128))
                w0[at] = ws[i, j] if 0 <= i else zero
                i = 2 + a - b
                w1[at] = ws[i, j] if i <= 2 else zero


def conv_rows(count, ll, w0, w1):
    m = 32 * count
    sides = jnp.concatenate([ll[0:4].reshape(4 * m, 768), ll[1:5].reshape(4 * m, 768)], axis=1)
    res = jnp.dot(sides, jnp.concatenate([w0[...], w1[...]], axis=0), preferred_element_type=F32)
    return [res[m * (R // 2):m * (R // 2) + m, 128 * (R % 2):128 * (R % 2) + 128].reshape(count, 32, 128)
            for R in range(8)]


def conv_kernel(
    pb_in, tb_in, ed_in, st_in, early, ends, ws_in, gain_in, bias_in, noise, out,
    st, gain, bias, pb, tb, ed, ws, nz, passing, passing_ends, r0, r1, r2, r3, r4, r5, r6,
    w0, w1, ll_a, ll_b, fld_a, fld_b, ea, qsem, nsem, osem, psem, wsem, ssem,
):
    f, r = lax.axis_index("frames"), lax.axis_index("rows")
    keeps = border_keeps(f, r)
    steps = 7
    res = (r0, r1, r2, r3, r4, r5, r6)

    def quad_loads(k):
        lo, n = ((0, 2), (2, 2), (4, 4))[k]
        at = pl.ds(lo, n)
        return [pltpu.make_async_copy(pb_in.at[at], pb.at[at], qsem.at[k, 0]),
                pltpu.make_async_copy(tb_in.at[:, at], tb.at[:, at], qsem.at[k, 1]),
                pltpu.make_async_copy(ed_in.at[:, at], ed.at[:, at], qsem.at[k, 2])]

    def frame_loads(k):
        return [pltpu.make_async_copy(noise.at[pl.ds(8 * g + 5, 5)], nz.at[g], nsem.at[g])
                for g in ((0, 1), (2, 3, 4, 5, 6))[k]]

    early_load = [pltpu.make_async_copy(early, passing, psem.at[0]), pltpu.make_async_copy(ends, passing_ends, psem.at[1])]
    early_store = [pltpu.make_async_copy(passing.at[q], out.at[pl.ds(8 * q + 2, 3)], psem.at[2 + q]) for q in range(8)]
    early_store += [pltpu.make_async_copy(passing_ends.at[pl.ds(0, 2)], out.at[pl.ds(0, 2)], psem.at[10]),
                    pltpu.make_async_copy(passing_ends.at[pl.ds(2, 3)], out.at[pl.ds(61, 3)], psem.at[11])]

    def stores(g):
        return [pltpu.make_async_copy(res[g], out.at[pl.ds(8 * g + 5, 5)], osem.at[g])]

    weights = pltpu.make_async_copy(ws_in, ws, wsem)
    small = [pltpu.make_async_copy(a, b, ssem.at[k]) for k, (a, b) in enumerate(
        ((st_in, st), (gain_in, gain), (bias_in, bias)))]
    for cp in small + quad_loads(0) + [weights]:
        cp.start()

    def step(g, new, old):
        if new is not None:
            ll, fld = new
            for i, (_, at, nxt) in enumerate(LATE):
                norm_frame(slot_of(g, at), nxt and slot_of(g, nxt), L_ROWS * g + i, i,
                           pb, tb, ed, st, gain, bias, ea.at[i], ll, fld, keeps)
        if old is not None:
            h = g - 1
            ll, fld = old
            rows = conv_rows(len(LATE), ll, w0, w1)
            for R in range(8):
                for i, (_, _, nxt) in enumerate(LATE):
                    v = fld[i, R].astype(F32) * (1.0 if nxt is None else 0.5)
                    res[h][i, R] = (rows[R][i] + v + 0.3 * nz[h, i, R].astype(F32)).astype(BF)

    a, b = (ll_a, fld_a), (ll_b, fld_b)
    def arrive(copies):
        for cp in copies:
            cp.wait()

    def start(copies):
        for cp in copies:
            cp.start()

    arrive(small + quad_loads(0))
    start(quad_loads(1) + frame_loads(0))
    step(0, a, None)
    arrive([weights])
    fill_weights(ws, w0, w1)
    for g in range(1, steps + 1):
        if g == 1:
            arrive(quad_loads(1) + frame_loads(0))
            start(quad_loads(2) + frame_loads(1) + early_load)
        if g == 3:
            arrive(quad_loads(2) + frame_loads(1))
        step(g, (a, b)[g % 2] if g < steps else None, (b, a)[g % 2])
        if g > 1:
            start(stores(g - 2))
        if g == 5:
            arrive(early_load)
            start(early_store)
    start(stores(steps - 1))
    arrive(early_store)
    for q in range(steps):
        arrive(stores(q))


EARLY = ((2, (0, 2), None), (3, (0, 2), (0, 3)), (4, (0, 3), None))
LATE = ((5, (0, 3), (1, 0)), (6, (1, 0), None), (7, (1, 0), (1, 1)), (8, (1, 1), None), (9, (1, 1), (1, 2)))
ENDS = (((0, 1), None), ((0, 1), (0, 2)), ((7, 3), (8, 0)), ((8, 0), None), ((8, 0), (8, 0)))
HALO_AT = ((0,), (1, 2, 3))
E_ROWS, L_ROWS = 4, 6


def slot_of(q, at):
    return q + at[0], at[1]


def move_kernel(
    video, wt_in, wp_in, ws_in, gain_in, bias_in, noise, pb_out, tb_out, ed_out, st_out, early_out, ends_out,
    wt, wp, ws, gain, bias, vv, inner, halo, relay, w3, si, so, pb, tb, eo, ed,
    st_e, s1e, r1e, s2e, r2e, stat_e, st_l, s1l, r1l, s2l, r2l,
    nz, w0, w1, ll, ea, res_e, nz_x, ll_x, res_x,
    lsem, ns, nr, hs, hr, ls, lr, is_, ir, os, or_, ts, tr, es, er, sem_e1, sem_e2, sem_l1, sem_l2, osem, wsem,
):
    f, r = lax.axis_index("frames"), lax.axis_index("rows")
    z, x, c = f // 8, (f // 2) % 4, f % 2
    chip = f // 2
    sgn = 2 * c - 1
    is_end = (f == 0) | (f == NF - 1)
    not_end = jnp.logical_not(is_end)
    outer_frame, inner_frame = c, 1 - c
    outer_dev = jnp.clip(f + sgn, 0, NF - 1)
    inner_dev = f + 1 - 2 * c

    def wait_in(ref, sem):
        pltpu.make_async_copy(ref, ref, sem).wait()

    def column(zz, xx):
        return pl.ds(pl.multiple_of(zz * 256 + xx * 64, 64), 64)

    def far_first(i):
        j = i // 2
        dx = jnp.where(j == 0, 2, jnp.where(j == 1, 1, jnp.where(j == 2, 3, 0)))
        return (z + 1 - i % 2) % 2, (x + dx) % 4

    def near_first(n, zz, xx, sg):
        dx = jnp.where(n < 4, jnp.where(n % 2 == 0, -sg, 0), jnp.where(n % 2 == 0, sg, 2 * sg))
        return (zz + 1 - (n // 2) % 2) % 2, (xx + dx + 4) % 4

    barrier = pltpu.get_barrier_semaphore()
    for k in range(NF - 1):
        pl.semaphore_signal(barrier, inc=1, device_id={"frames": peer(f, k)}, device_id_type=MESH)
    for k in range(1, NR):
        pl.semaphore_signal(barrier, inc=1, device_id={"rows": (r + k) % NR}, device_id_type=MESH)
    nz_loads = [pltpu.make_async_copy(noise.at[:, pl.ds(2, 3)], nz, osem.at[4]),
                pltpu.make_async_copy(noise.at[0, pl.ds(0, 2)], nz_x.at[pl.ds(0, 2)], osem.at[6]),
                pltpu.make_async_copy(noise.at[7, pl.ds(5, 3)], nz_x.at[pl.ds(2, 3)], osem.at[7])]
    for cp in nz_loads:
        cp.start()
    loads = [pltpu.make_async_copy(video.at[k], vv.at[k], lsem.at[k]) for k in range(2)]
    for cp in loads:
        cp.start()
    small = [pltpu.make_async_copy(a, b, wsem.at[k]) for k, (a, b) in enumerate(
        ((wt_in, wt), (wp_in, wp), (ws_in, ws), (gain_in, gain), (bias_in, bias)))]
    for cp in small:
        cp.start()
    for cp in small[:2]:
        cp.wait()
    w3[0:256] = wt[2 - 2 * c]
    w3[256:512] = wt[1]
    w3[512:768] = wt[2 * c]

    @pl.when(is_end)
    def _():
        halo[...] = jnp.zeros(halo.shape, BF)

    for axis_at, ref in ((r, tb), (f, ed)):
        count = NR if ref is tb else NF
        for side, edge in ((0, 0), (1, count - 1)):
            @pl.when(axis_at == edge)
            def _():
                ref[side] = jnp.zeros(ref.shape[1:], BF)

    pb[0, 0] = jnp.zeros(pb.shape[2:], BF)
    pb[8, 1] = jnp.zeros(pb.shape[2:], BF)
    st_e[...] = jnp.zeros(st_e.shape, F32)
    st_l[...] = jnp.zeros(st_l.shape, F32)
    pl.semaphore_wait(barrier, NF + NR - 2)

    is_mid = (f == NF // 2 - 1) | (f == NF // 2)

    def halo_copy(n):
        zz, xx = near_first(n, outer_dev // 8, (x + sgn + 4) % 4, -sgn)
        return pltpu.make_async_remote_copy(
            src_ref=video.at[:, :, column(zz, xx)], dst_ref=halo.at[n], send_sem=hs.at[n], recv_sem=hr.at[n],
            device_id={"frames": outer_dev}, device_id_type=MESH)

    def detour_copy(n):
        zz, xx = near_first(n, outer_dev // 8, (x + sgn + 4) % 4, -sgn)
        return pltpu.make_async_remote_copy(
            src_ref=video.at[:, :, column(zz, xx)], dst_ref=relay.at[n - 2], send_sem=ls.at[n - 2], recv_sem=lr.at[n - 2],
            device_id={"frames": jnp.where(f < NF // 2, NF - 1, 0)}, device_id_type=MESH)

    def relay_copy(n):
        return pltpu.make_async_remote_copy(
            src_ref=relay.at[n - 2], dst_ref=halo.at[n], send_sem=hs.at[n], recv_sem=hr.at[n],
            device_id={"frames": jnp.where(f < NF // 2, NF // 2 - 1, NF // 2)}, device_id_type=MESH)

    def inner_copy(i):
        zz, xx = far_first(i)
        return pltpu.make_async_remote_copy(
            src_ref=video.at[inner_frame, :, column(zz, xx)], dst_ref=inner.at[i], send_sem=ns.at[i], recv_sem=nr.at[i],
            device_id={"frames": inner_dev}, device_id_type=MESH)

    for i in range(8):
        inner_copy(i).start()

    def halo_start(blocks):
        for n in blocks:
            if n < 2:
                @pl.when(not_end)
                def _():
                    halo_copy(n).start()
            else:
                @pl.when(not_end & jnp.logical_not(is_mid))
                def _():
                    halo_copy(n).start()

    @pl.when(is_mid)
    def _():
        for n in (2, 3):
            detour_copy(n).start()

    halo_start(HALO_AT[0])

    for cp in loads:
        cp.wait()

    def inner_send(i, dc):
        zz, xx = far_first(i)
        dest = zz * 8 + xx * 2 + (c + dc) % 2
        slot = 2 * i + dc
        return pltpu.make_async_remote_copy(
            src_ref=si.at[i, (c + dc) % 2], dst_ref=pb.at[chip, 2 + c], send_sem=is_.at[slot], recv_sem=ir.at[slot],
            device_id={"frames": dest}, device_id_type=MESH)

    def inner_block(i, carry):
        zz, xx = far_first(i)
        wait_in(inner.at[i], nr.at[i])
        here = column(zz, xx)
        proj = temporal(inner[i], vv[inner_frame, :, here], vv[outer_frame, :, here], w3, wp)
        for h in range(2):
            si[i, h] = proj[:, h]
        inner_send(i, 1).start()

        @pl.when(i < 7)
        def _():
            inner_send(i, 0).start()

        return carry

    lax.fori_loop(0, 8, inner_block, 0)
    own_inner = pltpu.make_async_copy(si.at[7, c], pb.at[chip, 2 + c], lsem.at[0])
    own_inner.start()

    def outer_send(n, dc, alone):
        zz, xx = near_first(n, z, x, sgn)
        dest = zz * 8 + xx * 2 + (c + dc) % 2
        slot = 2 * n + dc
        src, dst = so.at[n, (c + dc) % 2], pb.at[chip + c]
        at = 1 - c if alone else pl.ds(0, 2)
        return pltpu.make_async_remote_copy(
            src_ref=src.at[at], dst_ref=dst.at[at], send_sem=os.at[slot], recv_sem=or_.at[slot],
            device_id={"frames": dest}, device_id_type=MESH)

    def outer_part(n, dc, act):
        @pl.when(is_end)
        def _():
            cp = outer_send(n, dc, True)
            cp.start() if act == "start" else cp.wait_send()

        if not (isinstance(n, int) and n > 3):
            @pl.when(not_end)
            def _():
                cp = outer_send(n, dc, False)
                cp.start() if act == "start" else cp.wait_send()

    def outer_block(n, carry):
        zz, xx = near_first(n, z, x, sgn)
        here = column(zz, xx)
        at = n % 4

        @pl.when(not_end)
        def _():
            wait_in(halo.at[at], hr.at[at])

        proj = temporal(vv[inner_frame, :, here], vv[outer_frame, :, here], halo[at, 1 - c], w3, wp)
        for h in range(2):
            so[n, h, 1 - c] = proj[:, h]

        @pl.when(not_end)
        def _():
            proj = temporal(vv[outer_frame, :, here], halo[at, 1 - c], halo[at, c], w3, wp)
            for h in range(2):
                so[n, h, c] = proj[:, h]

        outer_part(n, 1, "start")

        @pl.when(n != 3)
        def _():
            outer_part(n, 0, "start")

        return carry

    def outer_blocks(first, past):
        lax.fori_loop(first, past, outer_block, 0)

    halo_start(HALO_AT[1])

    @pl.when(is_end)
    def _():
        outer_blocks(4, 8)
        outer_blocks(0, 4)
        for n in (2, 3):
            wait_in(relay.at[n - 2], lr.at[n - 2])
            relay_copy(n).start()

    def blocks_not_end(first, past):
        @pl.when(not_end)
        def _():
            outer_blocks(first, past)

    blocks_not_end(0, 2)

    def both_ways(axis, at, up_refs, down_refs, ssem, rsem, base, act):
        count = lax.axis_size(axis)
        first, last = at == 0, at == count - 1
        up = pltpu.make_async_remote_copy(
            src_ref=up_refs[0], dst_ref=up_refs[1], send_sem=ssem.at[base], recv_sem=rsem.at[base],
            device_id={axis: jnp.maximum(at - 1, 0)}, device_id_type=MESH)
        down = pltpu.make_async_remote_copy(
            src_ref=down_refs[0], dst_ref=down_refs[1], send_sem=ssem.at[base + 1], recv_sem=rsem.at[base + 1],
            device_id={axis: jnp.minimum(at + 1, count - 1)}, device_id_type=MESH)

        @pl.when(jnp.logical_not(first))
        def _():
            if act == "start":
                up.start()
            else:
                up.wait_send()
                down.wait_recv()

        @pl.when(jnp.logical_not(last))
        def _():
            if act == "start":
                down.start()
            else:
                down.wait_send()
                up.wait_recv()

    def rows_copies(q, lo, base, act):
        part = (pl.ds(0, q), pl.ds(lo, 2))
        both_ways("rows", r, (pb.at[part + (0,)], tb.at[(1,) + part]), (pb.at[part + (7,)], tb.at[(0,) + part]), ts, tr, base, act)

    def pair_rows(q, act):
        part = (q, pl.ds(0, 2))
        both_ways("rows", r, (pb.at[part + (0,)], tb.at[(1,) + part]), (pb.at[part + (7,)], tb.at[(0,) + part]),
                  ts, tr, 2 + 2 * q, act)

    def side_copies(first, q, lo, base, act):
        part = (pl.ds(first, q), pl.ds(lo, 2))
        both_ways("frames", f, (eo.at[(0,) + part], ed.at[(1,) + part]), (eo.at[(1,) + part], ed.at[(0,) + part]), es, er, base, act)

    sub = lax.broadcasted_iota(jnp.int32, (8, 128), 0)

    def edges(lo):
        def body(q, carry):
            for k in (lo, lo + 1):
                for s in range(2):
                    cols = slice(16 * s, 16 * s + 16)
                    at = 15 * s
                    own = pb[q, k, :, cols].astype(F32)[:, at, :]
                    above = tb[0, q, k, cols].astype(F32)[at:at + 1]
                    below = tb[1, q, k, cols].astype(F32)[at:at + 1]
                    outside = jnp.where(sub == 0, above, below)
                    eo[s, q, k] = jnp.concatenate([own, outside], axis=0).astype(BF)
            return carry
        return body

    def add_sums(table, row, now, nxt):
        v = pb[now].reshape(256, 128)
        if nxt is not None:
            v = v + pb[nxt].reshape(256, 128)
        v = v.astype(F32)
        scale = 1.0 if nxt is None else 0.5
        row = pl.ds(row, 1)
        table[0, row] = scale * jnp.sum(v, axis=0, keepdims=True)
        table[1, row] = scale * scale * jnp.sum(v * v, axis=0, keepdims=True)

    def early_sums(q, carry):
        for i, (_, at, nxt) in enumerate(EARLY):
            add_sums(st_e, E_ROWS * q + i, slot_of(q, at), nxt and slot_of(q, nxt))
        return carry

    def pair_arrived(q):
        pair_rows(q, "start")
        for i, (_, at, nxt) in enumerate(LATE):
            add_sums(st_l, L_ROWS * (q - 1) + i, slot_of(q - 1, at), nxt and slot_of(q - 1, nxt))

    def source_of(slot):
        n, dc = slot // 2, slot % 2
        from_c = (c + dc) % 2
        sg = 2 * from_c - 1
        dx = jnp.where(n > 3, sg * (1 + n % 2), jnp.where(n % 2 == 0, -sg, 0))
        from_dev = ((z + 1 - (n // 2) % 2) % 2) * 8 + ((x - dx + 4) % 4) * 2 + from_c
        return from_dev, (from_dev == 0) | (from_dev == NF - 1)

    def end_arrival(slot, carry):
        @pl.when(source_of(slot)[1] & (slot != 6))
        def _():
            wait_in(pb.at[0, 0], or_.at[slot])
        return carry

    def outer_arrival(slot, carry):
        from_dev, from_end = source_of(slot)

        @pl.when(jnp.logical_not(from_end) & (slot != 6))
        def _():
            wait_in(pb.at[0, pl.ds(0, 2)], or_.at[slot])
            pair_arrived(from_dev // 2 + from_dev % 2)

        return carry

    def reduce_rows(table, s1, r1, sem):
        half = table.shape[1] // 2
        s1[...] = gather_groups([table[k // 2, half * (k % 2):half * (k % 2) + half] for k in range(4)])
        copies = []
        for k in range(1, NR):
            cp = pltpu.make_async_remote_copy(
                src_ref=s1, dst_ref=r1.at[k - 1], send_sem=sem.at[0, k - 1], recv_sem=sem.at[1, k - 1],
                device_id={"rows": (r + k) % NR}, device_id_type=MESH)
            cp.start()
            copies.append(cp)
        return copies

    def reduce_frames(copies, s1, r1, s2, r2, sem):
        for cp in copies:
            cp.wait()
        total = s1[...]
        for k in range(NR - 1):
            total += r1[k]
        s2[...] = total
        copies = []
        for k in range(NF - 1):
            cp = pltpu.make_async_remote_copy(
                src_ref=s2, dst_ref=r2.at[k], send_sem=sem.at[0, k], recv_sem=sem.at[1, k],
                device_id={"frames": peer(f, k)}, device_id_type=MESH)
            cp.start()
            copies.append(cp)
        return copies

    def statistics(copies, s2, r2, out):
        for cp in copies:
            cp.wait()
        total = s2[...]
        for k in range(NF - 1):
            total += r2[k]
        count = 64 * 512 * 4
        half = out.shape[1] // 2
        for k in range(2):
            mean = spread_groups(total, k) / count
            square = spread_groups(total, k + 2) / count
            out[0, half * k:half * k + half] = mean
            out[1, half * k:half * k + half] = lax.rsqrt(square - mean * mean + 1e-05)

    for i in range(8):
        for dc in range(2):
            if i < 7 or dc:
                wait_in(pb.at[0, 2], ir.at[2 * i + dc])
    own_inner.wait()
    rows_copies(8, 2, 0, "start")
    lax.fori_loop(0, 16, end_arrival, 0)

    @pl.when(is_end)
    def _():
        own_frame = pltpu.make_async_copy(so.at[3, c, 1 - c], pb.at[chip + c, 1 - c], lsem.at[1])
        own_frame.start()
        own_frame.wait()

    for q in (0, 8):
        pair_rows(q, "start")
    lax.fori_loop(0, 8, early_sums, 0)
    for i, (at, nxt) in enumerate(ENDS):
        add_sums(st_e, E_ROWS * i + 3, at, nxt)
    early_copies = reduce_rows(st_e, s1e, r1e, sem_e1)
    for cp in small[2:]:
        cp.wait()
    fill_weights(ws, w0, w1)
    blocks_not_end(2, 3)
    rows_copies(8, 2, 0, "wait")
    lax.fori_loop(0, 8, edges(2), 0)
    side_copies(0, 8, 2, 0, "start")
    for k, q in enumerate((0, 8)):
        pair_rows(q, "wait")
        edges(0)(q, 0)
        side_copies(q, 1, 0, 4 + 2 * k, "start")
    early_copies = reduce_frames(early_copies, s1e, r1e, s2e, r2e, sem_e2)
    blocks_not_end(3, 4)
    own_pair = pltpu.make_async_copy(so.at[3, c], pb.at[chip + c, pl.ds(0, 2)], lsem.at[1])

    @pl.when(not_end)
    def _():
        own_pair.start()


    lax.fori_loop(0, 8, outer_arrival, 0)

    @pl.when(not_end)
    def _():
        own_pair.wait()
        pair_arrived(chip + c)

    late_copies = reduce_rows(st_l, s1l, r1l, sem_l1)
    pb_copy = pltpu.make_async_copy(pb, pb_out, osem.at[0])
    pb_copy.start()
    side_copies(0, 8, 2, 0, "wait")
    for k, q in enumerate((0, 8)):
        side_copies(q, 1, 0, 4 + 2 * k, "wait")
    for cp in nz_loads:
        cp.wait()
    statistics(early_copies, s2e, r2e, stat_e)

    keeps = border_keeps(f, r)

    def early_conv(q, carry):
        for i, (_, at, nxt) in enumerate(EARLY):
            norm_frame(slot_of(q, at), nxt and slot_of(q, nxt), E_ROWS * q + i, i,
                       pb, tb, ed, stat_e, gain, bias, ea.at[i], ll, None, keeps)
        rows = conv_rows(3, ll, w0, w1)
        for R in range(8):
            for i, (_, at, nxt) in enumerate(EARLY):
                v = pb[q, at[1], R]
                if nxt is not None:
                    v = v + pb[q, nxt[1], R]
                v = v.astype(F32) * (1.0 if nxt is None else 0.5)
                res_e[q, i, R] = (rows[R][i] + v + 0.3 * nz[q, i, R].astype(F32)).astype(BF)
        return carry

    lax.fori_loop(0, 4, early_conv, 0)
    late_copies = reduce_frames(late_copies, s1l, r1l, s2l, r2l, sem_l2)
    for q in range(1, 8):
        pair_rows(q, "wait")
    lax.fori_loop(1, 8, edges(0), 0)
    side_copies(1, 7, 0, 2, "start")
    tb_copy = pltpu.make_async_copy(tb, tb_out, osem.at[1])
    tb_copy.start()
    lax.fori_loop(4, 8, early_conv, 0)
    for i, (at, nxt) in enumerate(ENDS):
        norm_frame(at, nxt, E_ROWS * i + 3, i, pb, tb, ed, stat_e, gain, bias, ea.at[i], ll_x, None, keeps)
    rows = conv_rows(5, ll_x, w0, w1)
    for R in range(8):
        for i, (at, nxt) in enumerate(ENDS):
            v = pb[at[0], at[1], R]
            if nxt is not None:
                v = v + pb[nxt[0], nxt[1], R]
            v = v.astype(F32) * (1.0 if nxt is None else 0.5)
            res_x[i, R] = (rows[R][i] + v + 0.3 * nz_x[i, R].astype(F32)).astype(BF)
    early_copy = pltpu.make_async_copy(res_e, early_out, osem.at[3])
    early_copy.start()
    ends_copy = pltpu.make_async_copy(res_x, ends_out, osem.at[5])
    ends_copy.start()

    for i in range(8):
        inner_copy(i).wait_send()
        inner_send(i, 1).wait_send()
        if i < 7:
            inner_send(i, 0).wait_send()
    for n in range(4):
        outer_part(n, 1, "wait")
        if n != 3:
            outer_part(n, 0, "wait")

    @pl.when(not_end)
    def _():
        for n in range(2):
            halo_copy(n).wait_send()

    for n in range(2, 4):
        @pl.when(is_mid)
        def _():
            detour_copy(n).wait_send()

        @pl.when(jnp.logical_not(is_mid))
        def _():
            halo_copy(n).wait_send()

    @pl.when(is_end)
    def _():
        for n in range(4, 8):
            outer_send(n, 1, True).wait_send()
            outer_send(n, 0, True).wait_send()

    side_copies(1, 7, 0, 2, "wait")
    ed_copy = pltpu.make_async_copy(ed, ed_out, osem.at[2])
    ed_copy.start()
    statistics(late_copies, s2l, r2l, st_out)
    pb_copy.wait()
    tb_copy.wait()
    ed_copy.wait()
    early_copy.wait()
    ends_copy.wait()


def local(video, w_time, w_proj, w_space, gn_gain, gn_bias, noise):
    slots = 2 * NF + 4
    anyw = pl.BlockSpec(memory_space=pl.ANY)
    vm = pl.BlockSpec(memory_space=pltpu.VMEM)
    quads = slots // 4
    dma = pltpu.SemaphoreType.DMA
    gain, bias = gn_gain.reshape(1, 128), gn_bias.reshape(1, 128)
    noise = noise.reshape(8, 8, 8, 32, 128)
    pb, tb, ed, st, early, ends = pl.pallas_call(
        move_kernel,
        out_shape=(
            jax.ShapeDtypeStruct((quads, 4, 8, 32, 128), BF),
            jax.ShapeDtypeStruct((2, quads, 4, 32, 128), BF),
            jax.ShapeDtypeStruct((2, quads, 4, 16, 128), BF),
            jax.ShapeDtypeStruct((2, 8 * L_ROWS, 128), F32),
            jax.ShapeDtypeStruct((8, 3, 8, 32, 128), BF),
            jax.ShapeDtypeStruct((5, 8, 32, 128), BF),
        ),
        in_specs=[anyw, anyw, anyw, anyw, anyw, anyw, anyw],
        out_specs=(anyw, anyw, anyw, vm, anyw, anyw),
        scratch_shapes=[
            pltpu.VMEM((3, 256, 256), BF),
            pltpu.VMEM((256, 128), BF),
            pltpu.VMEM((3, 3, 128, 128), BF),
            pltpu.VMEM((1, 128), F32),
            pltpu.VMEM((1, 128), F32),
            pltpu.VMEM((2, 8, 512, 256), BF),
            pltpu.VMEM((8, 8, 64, 256), BF),
            pltpu.VMEM((4, 2, 8, 64, 256), BF),
            pltpu.VMEM((2, 2, 8, 64, 256), BF),
            pltpu.VMEM((768, 256), BF),
            pltpu.VMEM((8, 2, 8, 32, 128), BF),
            pltpu.VMEM((8, 2, 2, 8, 32, 128), BF),
            pltpu.VMEM((quads, 4, 8, 32, 128), BF),
            pltpu.VMEM((2, quads, 4, 32, 128), BF),
            pltpu.VMEM((2, quads, 4, 16, 128), BF),
            pltpu.VMEM((2, quads, 4, 16, 128), BF),
            pltpu.VMEM((2, 8 * E_ROWS, 128), F32),
            pltpu.VMEM((4 * E_ROWS, 128), F32),
            pltpu.VMEM((NR - 1, 4 * E_ROWS, 128), F32),
            pltpu.VMEM((4 * E_ROWS, 128), F32),
            pltpu.VMEM((NF - 1, 4 * E_ROWS, 128), F32),
            pltpu.VMEM((2, 8 * E_ROWS, 128), F32),
            pltpu.VMEM((2, 8 * L_ROWS, 128), F32),
            pltpu.VMEM((4 * L_ROWS, 128), F32),
            pltpu.VMEM((NR - 1, 4 * L_ROWS, 128), F32),
            pltpu.VMEM((4 * L_ROWS, 128), F32),
            pltpu.VMEM((NF - 1, 4 * L_ROWS, 128), F32),
            pltpu.VMEM((8, 3, 8, 32, 128), BF),
            pltpu.VMEM((768, 256), BF),
            pltpu.VMEM((768, 256), BF),
            pltpu.VMEM((5, 96, 768), BF),
            pltpu.VMEM((5, 2, 16, 128), F32),
            pltpu.VMEM((8, 3, 8, 32, 128), BF),
            pltpu.VMEM((5, 8, 32, 128), BF),
            pltpu.VMEM((5, 160, 768), BF),
            pltpu.VMEM((5, 8, 32, 128), BF),
            dma((2,)),
            dma((8,)), dma((8,)),
            dma((4,)), dma((4,)),
            dma((2,)), dma((2,)),
            dma((16,)), dma((16,)),
            dma((16,)), dma((16,)),
            dma((20,)), dma((20,)),
            dma((8,)), dma((8,)),
            dma((2, NR - 1)), dma((2, NF - 1)),
            dma((2, NR - 1)), dma((2, NF - 1)),
            dma((8,)),
            dma((5,)),
        ],
        compiler_params=pltpu.CompilerParams(collective_id=0, has_side_effects=True, vmem_limit_bytes=60 << 20),
        name="move",
    )(video, w_time, w_proj, w_space, gain, bias, noise)
    out = pl.pallas_call(
        conv_kernel,
        out_shape=jax.ShapeDtypeStruct((64, 8, 32, 128), BF),
        in_specs=[anyw] * 10,
        out_specs=anyw,
        scratch_shapes=[
            pltpu.VMEM((2, 8 * L_ROWS, 128), F32),
            pltpu.VMEM((1, 128), F32),
            pltpu.VMEM((1, 128), F32),
            pltpu.VMEM((quads, 4, 8, 32, 128), BF),
            pltpu.VMEM((2, quads, 4, 32, 128), BF),
            pltpu.VMEM((2, quads, 4, 16, 128), BF),
            pltpu.VMEM((3, 3, 128, 128), BF),
            pltpu.VMEM((8, 5, 8, 32, 128), BF),
            pltpu.VMEM((8, 3, 8, 32, 128), BF),
            *[pltpu.VMEM((5, 8, 32, 128), BF)] * 8,
            pltpu.VMEM((768, 256), BF),
            pltpu.VMEM((768, 256), BF),
            pltpu.VMEM((5, 160, 768), BF),
            pltpu.VMEM((5, 160, 768), BF),
            pltpu.VMEM((5, 8, 32, 128), BF),
            pltpu.VMEM((5, 8, 32, 128), BF),
            pltpu.VMEM((5, 2, 16, 128), F32),
            dma((3, 3)), dma((7,)), dma((7,)), dma((12,)), dma, dma((3,)),
        ],
        compiler_params=pltpu.CompilerParams(vmem_limit_bytes=60 << 20),
        name="conv",
    )(pb, tb, ed, st, early, ends, w_space, gain, bias, noise.reshape(64, 8, 32, 128))
    return out


def solution(mesh):
    in_specs = (
        P("frames", "rows", None, None),
        P(), P(), P(), P(), P(),
        P(None, "rows", "frames", None),
    )
    out_specs = P(None, "rows", "frames", None)
    return jax.shard_map(local, mesh=mesh, in_specs=in_specs, out_specs=out_specs, check_vma=False)
```

```python
import jax
import jax.numpy as jnp
from jax import lax
from jax.experimental import pallas as pl
from jax.experimental.pallas import tpu as pltpu
from jax.sharding import PartitionSpec as P

MESH = pl.DeviceIdType.MESH
NF, NR = 16, 8
GROUPS = 32
BF, F32 = jnp.bfloat16, jnp.float32

PEERS = [(dz, dx, dc) for dx in (2, 1, 3, 0) for dz in (1, 0) for dc in (0, 1) if (dz, dx, dc) != (0, 0, 0)]


def peer(f, k):
    dz, dx, dc = PEERS[k]
    z, x, c = f // 8, (f // 2) % 4, f % 2
    return ((z + dz) % 2) * 8 + ((x + dx) % 4) * 2 + (c + dc) % 2


def silu(v):
    h = 0.5 * v
    return h + h * jnp.tanh(h)


def gather_groups(parts):
    lane = lax.broadcasted_iota(jnp.int32, parts[0].shape, 1) & 3
    out = jnp.zeros(parts[0].shape, F32)
    for k, v in enumerate(parts):
        v = v + pltpu.roll(v, 127, 1)
        v = v + pltpu.roll(v, 126, 1)
        out = jnp.where(lane == k, pltpu.roll(v, k, 1) if k else v, out)
    return out


def spread_groups(v, k):
    lane = lax.broadcasted_iota(jnp.int32, v.shape, 1) & 3
    v = jnp.where(lane == k, v, 0.0)
    v = pltpu.roll(v, 128 - k, 1) if k else v
    v = v + pltpu.roll(v, 1, 1)
    return v + pltpu.roll(v, 2, 1)


def temporal(before, now, after, w3, wp):
    x = [v.reshape(512, 256) for v in (before, now, after)]
    taps = jnp.dot(jnp.concatenate(x, axis=1), w3[...], preferred_element_type=F32)
    mixed = (x[1].astype(F32) + silu(taps)).astype(BF)
    proj = jnp.dot(mixed, wp[...], preferred_element_type=F32).astype(BF)
    return proj.reshape(8, 2, 32, 128)


def border_keeps(f, r):
    return (jnp.where(r > 0, 1.0, 0.0), jnp.where(r < NR - 1, 1.0, 0.0),
            (jnp.where(f > 0, 1.0, 0.0), jnp.where(f < NF - 1, 1.0, 0.0)))


def norm_frame(now, nxt, line, place, pb, tb, ed, st, gain, bias, ea, ll, fld, keeps):
    keep_top, keep_bottom, keep_side = keeps
    line = pl.ds(line, 1)
    scale = st[1, line] * gain[...]
    shift = 0.5 * (bias[...] - st[0, line] * scale)
    scale = (0.5 if nxt is None else 0.25) * scale
    sub = lax.broadcasted_iota(jnp.int32, (8, 128), 0)

    def act_of(ref, before, after, keep=None):
        v = ref[before + now + after]
        if nxt is not None:
            v = v + ref[before + nxt + after]
        if keep is not None:
            keep[...] = v
        h = v.astype(F32) * scale + shift
        return h + h * jnp.tanh(h)

    for s in range(2):
        ea[s] = act_of(ed, (s,), ()) * keep_side[s]
    for R in range(10):
        E = 8 if R == 0 else R - 1 if R < 9 else 9
        el, er = ea[0, E:E + 1], ea[1, E:E + 1]
        if R == 0:
            a = act_of(tb, (0,), ()) * keep_top
            el, er = el * keep_top, er * keep_top
        elif R == 9:
            a = act_of(tb, (1,), ()) * keep_bottom
            el, er = el * keep_bottom, er * keep_bottom
        else:
            a = act_of(pb, (), (R - 1,), None if fld is None else fld.at[place, R - 1])
        tiles = [a[8 * i:8 * i + 8] for i in range(4)]
        down = [pltpu.roll(v, 1, 0) for v in tiles]
        up = [pltpu.roll(v, 7, 0) for v in tiles]
        left = [jnp.where(sub == 0, down[i - 1] if i else el, down[i]) for i in range(4)]
        right = [jnp.where(sub == 7, up[i + 1] if i < 3 else er, up[i]) for i in range(4)]
        for j, v in enumerate((jnp.concatenate(left, 0), a, jnp.concatenate(right, 0))):
            lane = 256 * j + 128 * (R % 2)
            ll[R // 2, 32 * place:32 * place + 32, lane:lane + 128] = v.astype(BF)


def fill_weights(ws, w0, w1):
    zero = jnp.zeros((128, 128), BF)
    for j in range(3):
        for a in range(2):
            for b in range(2):
                i = a - b
                at = (slice(256 * j + 128 * a, 256 * j + 128 * a + 128), slice(128 * b, 128 * b + 128))
                w0[at] = ws[i, j] if 0 <= i else zero
                i = 2 + a - b
                w1[at] = ws[i, j] if i <= 2 else zero


def conv_rows(count, ll, w0, w1):
    m = 32 * count
    sides = jnp.concatenate([ll[0:4].reshape(4 * m, 768), ll[1:5].reshape(4 * m, 768)], axis=1)
    res = jnp.dot(sides, jnp.concatenate([w0[...], w1[...]], axis=0), preferred_element_type=F32)
    return [res[m * (R // 2):m * (R // 2) + m, 128 * (R % 2):128 * (R % 2) + 128].reshape(count, 32, 128)
            for R in range(8)]


def conv_kernel(
    pb_in, tb_in, ed_in, st_in, early, ends, ws_in, gain_in, bias_in, noise, out,
    st, gain, bias, pb, tb, ed, ws, nz, passing, passing_ends, r0, r1, r2, r3, r4, r5, r6,
    w0, w1, ll_a, ll_b, fld_a, fld_b, ea, qsem, nsem, osem, psem, wsem, ssem,
):
    f, r = lax.axis_index("frames"), lax.axis_index("rows")
    keeps = border_keeps(f, r)
    steps = 7
    res = (r0, r1, r2, r3, r4, r5, r6)

    def quad_loads(k):
        lo, n = ((0, 2), (2, 2), (4, 4))[k]
        at = pl.ds(lo, n)
        return [pltpu.make_async_copy(pb_in.at[at], pb.at[at], qsem.at[k, 0]),
                pltpu.make_async_copy(tb_in.at[:, at], tb.at[:, at], qsem.at[k, 1]),
                pltpu.make_async_copy(ed_in.at[:, at], ed.at[:, at], qsem.at[k, 2])]

    def frame_loads(k):
        return [pltpu.make_async_copy(noise.at[pl.ds(8 * g + 5, 5)], nz.at[g], nsem.at[g])
                for g in ((0, 1), (2, 3, 4, 5, 6))[k]]

    early_load = [pltpu.make_async_copy(early, passing, psem.at[0]), pltpu.make_async_copy(ends, passing_ends, psem.at[1])]
    early_store = [pltpu.make_async_copy(passing.at[q], out.at[pl.ds(8 * q + 2, 3)], psem.at[2 + q]) for q in range(8)]
    early_store += [pltpu.make_async_copy(passing_ends.at[pl.ds(0, 2)], out.at[pl.ds(0, 2)], psem.at[10]),
                    pltpu.make_async_copy(passing_ends.at[pl.ds(2, 3)], out.at[pl.ds(61, 3)], psem.at[11])]

    def stores(g):
        return [pltpu.make_async_copy(res[g], out.at[pl.ds(8 * g + 5, 5)], osem.at[g])]

    weights = pltpu.make_async_copy(ws_in, ws, wsem)
    small = [pltpu.make_async_copy(a, b, ssem.at[k]) for k, (a, b) in enumerate(
        ((st_in, st), (gain_in, gain), (bias_in, bias)))]
    for cp in small + quad_loads(0) + [weights]:
        cp.start()

    def step(g, new, old):
        if new is not None:
            ll, fld = new
            for i, (_, at, nxt) in enumerate(LATE):
                norm_frame(slot_of(g, at), nxt and slot_of(g, nxt), L_ROWS * g + i, i,
                           pb, tb, ed, st, gain, bias, ea.at[i], ll, fld, keeps)
        if old is not None:
            h = g - 1
            ll, fld = old
            rows = conv_rows(len(LATE), ll, w0, w1)
            for R in range(8):
                for i, (_, _, nxt) in enumerate(LATE):
                    v = fld[i, R].astype(F32) * (1.0 if nxt is None else 0.5)
                    res[h][i, R] = (rows[R][i] + v + 0.3 * nz[h, i, R].astype(F32)).astype(BF)

    a, b = (ll_a, fld_a), (ll_b, fld_b)
    def arrive(copies):
        for cp in copies:
            cp.wait()

    def start(copies):
        for cp in copies:
            cp.start()

    arrive(small + quad_loads(0))
    start(quad_loads(1) + frame_loads(0))
    step(0, a, None)
    arrive([weights])
    fill_weights(ws, w0, w1)
    for g in range(1, steps + 1):
        if g == 1:
            arrive(quad_loads(1) + frame_loads(0))
            start(quad_loads(2) + frame_loads(1) + early_load)
        if g == 3:
            arrive(quad_loads(2) + frame_loads(1))
        step(g, (a, b)[g % 2] if g < steps else None, (b, a)[g % 2])
        if g > 1:
            start(stores(g - 2))
        if g == 5:
            arrive(early_load)
            start(early_store)
    start(stores(steps - 1))
    arrive(early_store)
    for q in range(steps):
        arrive(stores(q))


EARLY = ((2, (0, 2), None), (3, (0, 2), (0, 3)), (4, (0, 3), None))
LATE = ((5, (0, 3), (1, 0)), (6, (1, 0), None), (7, (1, 0), (1, 1)), (8, (1, 1), None), (9, (1, 1), (1, 2)))
ENDS = (((0, 1), None), ((0, 1), (0, 2)), ((7, 3), (8, 0)), ((8, 0), None), ((8, 0), (8, 0)))
HALO_AT = ((0,), (1, 2, 3))
E_ROWS, L_ROWS = 4, 6


def slot_of(q, at):
    return q + at[0], at[1]


def move_kernel(
    video, wt_in, wp_in, ws_in, gain_in, bias_in, noise, pb_out, tb_out, ed_out, st_out, early_out, ends_out,
    wt, wp, ws, gain, bias, vv, inner, halo, relay, w3, si, so, pb, tb, eo, ed,
    st_e, s1e, r1e, s2e, r2e, stat_e, st_l, s1l, r1l, s2l, r2l,
    nz, w0, w1, ll, ea, res_e, nz_x, ll_x, res_x,
    lsem, ns, nr, hs, hr, ls, lr, is_, ir, os, or_, ts, tr, es, er, sem_e1, sem_e2, sem_l1, sem_l2, osem, wsem,
):
    f, r = lax.axis_index("frames"), lax.axis_index("rows")
    z, x, c = f // 8, (f // 2) % 4, f % 2
    chip = f // 2
    sgn = 2 * c - 1
    is_end = (f == 0) | (f == NF - 1)
    not_end = jnp.logical_not(is_end)
    outer_frame, inner_frame = c, 1 - c
    outer_dev = jnp.clip(f + sgn, 0, NF - 1)
    inner_dev = f + 1 - 2 * c

    def wait_in(ref, sem):
        pltpu.make_async_copy(ref, ref, sem).wait()

    def column(zz, xx):
        return pl.ds(pl.multiple_of(zz * 256 + xx * 64, 64), 64)

    def far_first(i):
        j = i // 2
        dx = jnp.where(j == 0, 2, jnp.where(j == 1, 1, jnp.where(j == 2, 3, 0)))
        return (z + 1 - i % 2) % 2, (x + dx) % 4

    def near_first(n, zz, xx, sg):
        dx = jnp.where(n < 4, jnp.where(n % 2 == 0, -sg, 0), jnp.where(n % 2 == 0, sg, 2 * sg))
        return (zz + 1 - (n // 2) % 2) % 2, (xx + dx + 4) % 4

    barrier = pltpu.get_barrier_semaphore()
    for k in range(NF - 1):
        pl.semaphore_signal(barrier, inc=1, device_id={"frames": peer(f, k)}, device_id_type=MESH)
    for k in range(1, NR):
        pl.semaphore_signal(barrier, inc=1, device_id={"rows": (r + k) % NR}, device_id_type=MESH)
    nz_loads = [pltpu.make_async_copy(noise.at[:, pl.ds(2, 3)], nz, osem.at[4]),
                pltpu.make_async_copy(noise.at[0, pl.ds(0, 2)], nz_x.at[pl.ds(0, 2)], osem.at[6]),
                pltpu.make_async_copy(noise.at[7, pl.ds(5, 3)], nz_x.at[pl.ds(2, 3)], osem.at[7])]
    for cp in nz_loads:
        cp.start()
    loads = [pltpu.make_async_copy(video.at[k], vv.at[k], lsem.at[k]) for k in range(2)]
    for cp in loads:
        cp.start()
    small = [pltpu.make_async_copy(a, b, wsem.at[k]) for k, (a, b) in enumerate(
        ((wt_in, wt), (wp_in, wp), (ws_in, ws), (gain_in, gain), (bias_in, bias)))]
    for cp in small:
        cp.start()
    for cp in small[:2]:
        cp.wait()
    w3[0:256] = wt[2 - 2 * c]
    w3[256:512] = wt[1]
    w3[512:768] = wt[2 * c]

    @pl.when(is_end)
    def _():
        halo[...] = jnp.zeros(halo.shape, BF)

    for axis_at, ref in ((r, tb), (f, ed)):
        count = NR if ref is tb else NF
        for side, edge in ((0, 0), (1, count - 1)):
            @pl.when(axis_at == edge)
            def _():
                ref[side] = jnp.zeros(ref.shape[1:], BF)

    pb[0, 0] = jnp.zeros(pb.shape[2:], BF)
    pb[8, 1] = jnp.zeros(pb.shape[2:], BF)
    st_e[...] = jnp.zeros(st_e.shape, F32)
    st_l[...] = jnp.zeros(st_l.shape, F32)
    pl.semaphore_wait(barrier, NF + NR - 2)

    is_mid = (f == NF // 2 - 1) | (f == NF // 2)

    def halo_copy(n):
        zz, xx = near_first(n, outer_dev // 8, (x + sgn + 4) % 4, -sgn)
        return pltpu.make_async_remote_copy(
            src_ref=video.at[:, :, column(zz, xx)], dst_ref=halo.at[n], send_sem=hs.at[n], recv_sem=hr.at[n],
            device_id={"frames": outer_dev}, device_id_type=MESH)

    def detour_copy(n):
        zz, xx = near_first(n, outer_dev // 8, (x + sgn + 4) % 4, -sgn)
        return pltpu.make_async_remote_copy(
            src_ref=video.at[:, :, column(zz, xx)], dst_ref=relay.at[n - 2], send_sem=ls.at[n - 2], recv_sem=lr.at[n - 2],
            device_id={"frames": jnp.where(f < NF // 2, NF - 1, 0)}, device_id_type=MESH)

    def relay_copy(n):
        return pltpu.make_async_remote_copy(
            src_ref=relay.at[n - 2], dst_ref=halo.at[n], send_sem=hs.at[n], recv_sem=hr.at[n],
            device_id={"frames": jnp.where(f < NF // 2, NF // 2 - 1, NF // 2)}, device_id_type=MESH)

    def inner_copy(i):
        zz, xx = far_first(i)
        return pltpu.make_async_remote_copy(
            src_ref=video.at[inner_frame, :, column(zz, xx)], dst_ref=inner.at[i], send_sem=ns.at[i], recv_sem=nr.at[i],
            device_id={"frames": inner_dev}, device_id_type=MESH)

    for i in range(8):
        inner_copy(i).start()

    def halo_start(blocks):
        for n in blocks:
            if n < 2:
                @pl.when(not_end)
                def _():
                    halo_copy(n).start()
            else:
                @pl.when(not_end & jnp.logical_not(is_mid))
                def _():
                    halo_copy(n).start()

    @pl.when(is_mid)
    def _():
        for n in (2, 3):
            detour_copy(n).start()

    halo_start(HALO_AT[0])

    for cp in loads:
        cp.wait()

    def inner_send(i, dc):
        zz, xx = far_first(i)
        dest = zz * 8 + xx * 2 + (c + dc) % 2
        slot = 2 * i + dc
        return pltpu.make_async_remote_copy(
            src_ref=si.at[i, (c + dc) % 2], dst_ref=pb.at[chip, 2 + c], send_sem=is_.at[slot], recv_sem=ir.at[slot],
            device_id={"frames": dest}, device_id_type=MESH)

    def inner_block(i, carry):
        zz, xx = far_first(i)
        wait_in(inner.at[i], nr.at[i])
        here = column(zz, xx)
        proj = temporal(inner[i], vv[inner_frame, :, here], vv[outer_frame, :, here], w3, wp)
        for h in range(2):
            si[i, h] = proj[:, h]
        inner_send(i, 1).start()

        @pl.when(i < 7)
        def _():
            inner_send(i, 0).start()

        return carry

    lax.fori_loop(0, 8, inner_block, 0)
    own_inner = pltpu.make_async_copy(si.at[7, c], pb.at[chip, 2 + c], lsem.at[0])
    own_inner.start()

    def outer_send(n, dc, alone):
        zz, xx = near_first(n, z, x, sgn)
        dest = zz * 8 + xx * 2 + (c + dc) % 2
        slot = 2 * n + dc
        src, dst = so.at[n, (c + dc) % 2], pb.at[chip + c]
        at = 1 - c if alone else pl.ds(0, 2)
        return pltpu.make_async_remote_copy(
            src_ref=src.at[at], dst_ref=dst.at[at], send_sem=os.at[slot], recv_sem=or_.at[slot],
            device_id={"frames": dest}, device_id_type=MESH)

    def outer_part(n, dc, act):
        @pl.when(is_end)
        def _():
            cp = outer_send(n, dc, True)
            cp.start() if act == "start" else cp.wait_send()

        if not (isinstance(n, int) and n > 3):
            @pl.when(not_end)
            def _():
                cp = outer_send(n, dc, False)
                cp.start() if act == "start" else cp.wait_send()

    def outer_block(n, carry):
        zz, xx = near_first(n, z, x, sgn)
        here = column(zz, xx)
        at = n % 4

        @pl.when(not_end)
        def _():
            wait_in(halo.at[at], hr.at[at])

        proj = temporal(vv[inner_frame, :, here], vv[outer_frame, :, here], halo[at, 1 - c], w3, wp)
        for h in range(2):
            so[n, h, 1 - c] = proj[:, h]

        @pl.when(not_end)
        def _():
            proj = temporal(vv[outer_frame, :, here], halo[at, 1 - c], halo[at, c], w3, wp)
            for h in range(2):
                so[n, h, c] = proj[:, h]

        outer_part(n, 1, "start")

        @pl.when(n != 3)
        def _():
            outer_part(n, 0, "start")

        return carry

    def outer_blocks(first, past):
        lax.fori_loop(first, past, outer_block, 0)

    halo_start(HALO_AT[1])

    @pl.when(is_end)
    def _():
        outer_blocks(4, 8)
        outer_blocks(0, 4)
        for n in (2, 3):
            wait_in(relay.at[n - 2], lr.at[n - 2])
            relay_copy(n).start()

    def blocks_not_end(first, past):
        @pl.when(not_end)
        def _():
            outer_blocks(first, past)

    blocks_not_end(0, 2)

    def both_ways(axis, at, up_refs, down_refs, ssem, rsem, base, act):
        count = lax.axis_size(axis)
        first, last = at == 0, at == count - 1
        up = pltpu.make_async_remote_copy(
            src_ref=up_refs[0], dst_ref=up_refs[1], send_sem=ssem.at[base], recv_sem=rsem.at[base],
            device_id={axis: jnp.maximum(at - 1, 0)}, device_id_type=MESH)
        down = pltpu.make_async_remote_copy(
            src_ref=down_refs[0], dst_ref=down_refs[1], send_sem=ssem.at[base + 1], recv_sem=rsem.at[base + 1],
            device_id={axis: jnp.minimum(at + 1, count - 1)}, device_id_type=MESH)

        @pl.when(jnp.logical_not(first))
        def _():
            if act == "start":
                up.start()
            else:
                up.wait_send()
                down.wait_recv()

        @pl.when(jnp.logical_not(last))
        def _():
            if act == "start":
                down.start()
            else:
                down.wait_send()
                up.wait_recv()

    def rows_copies(q, lo, base, act):
        part = (pl.ds(0, q), pl.ds(lo, 2))
        both_ways("rows", r, (pb.at[part + (0,)], tb.at[(1,) + part]), (pb.at[part + (7,)], tb.at[(0,) + part]), ts, tr, base, act)

    def pair_rows(q, act):
        part = (q, pl.ds(0, 2))
        both_ways("rows", r, (pb.at[part + (0,)], tb.at[(1,) + part]), (pb.at[part + (7,)], tb.at[(0,) + part]),
                  ts, tr, 2 + 2 * q, act)

    def side_copies(first, q, lo, base, act):
        part = (pl.ds(first, q), pl.ds(lo, 2))
        both_ways("frames", f, (eo.at[(0,) + part], ed.at[(1,) + part]), (eo.at[(1,) + part], ed.at[(0,) + part]), es, er, base, act)

    sub = lax.broadcasted_iota(jnp.int32, (8, 128), 0)

    def edges(lo):
        def body(q, carry):
            for k in (lo, lo + 1):
                for s in range(2):
                    cols = slice(16 * s, 16 * s + 16)
                    at = 15 * s
                    own = pb[q, k, :, cols].astype(F32)[:, at, :]
                    above = tb[0, q, k, cols].astype(F32)[at:at + 1]
                    below = tb[1, q, k, cols].astype(F32)[at:at + 1]
                    outside = jnp.where(sub == 0, above, below)
                    eo[s, q, k] = jnp.concatenate([own, outside], axis=0).astype(BF)
            return carry
        return body

    def add_sums(table, row, now, nxt):
        v = pb[now].reshape(256, 128)
        if nxt is not None:
            v = v + pb[nxt].reshape(256, 128)
        v = v.astype(F32)
        scale = 1.0 if nxt is None else 0.5
        row = pl.ds(row, 1)
        table[0, row] = scale * jnp.sum(v, axis=0, keepdims=True)
        table[1, row] = scale * scale * jnp.sum(v * v, axis=0, keepdims=True)

    def early_sums(q, carry):
        for i, (_, at, nxt) in enumerate(EARLY):
            add_sums(st_e, E_ROWS * q + i, slot_of(q, at), nxt and slot_of(q, nxt))
        return carry

    def pair_arrived(q):
        pair_rows(q, "start")
        for i, (_, at, nxt) in enumerate(LATE):
            add_sums(st_l, L_ROWS * (q - 1) + i, slot_of(q - 1, at), nxt and slot_of(q - 1, nxt))

    def source_of(slot):
        n, dc = slot // 2, slot % 2
        from_c = (c + dc) % 2
        sg = 2 * from_c - 1
        dx = jnp.where(n > 3, sg * (1 + n % 2), jnp.where(n % 2 == 0, -sg, 0))
        from_dev = ((z + 1 - (n // 2) % 2) % 2) * 8 + ((x - dx + 4) % 4) * 2 + from_c
        return from_dev, (from_dev == 0) | (from_dev == NF - 1)

    def end_arrival(slot, carry):
        @pl.when(source_of(slot)[1] & (slot != 6))
        def _():
            wait_in(pb.at[0, 0], or_.at[slot])
        return carry

    def outer_arrival(slot, carry):
        from_dev, from_end = source_of(slot)

        @pl.when(jnp.logical_not(from_end) & (slot != 6))
        def _():
            wait_in(pb.at[0, pl.ds(0, 2)], or_.at[slot])
            pair_arrived(from_dev // 2 + from_dev % 2)

        return carry

    def reduce_rows(table, s1, r1, sem):
        half = table.shape[1] // 2
        s1[...] = gather_groups([table[k // 2, half * (k % 2):half * (k % 2) + half] for k in range(4)])
        copies = []
        for k in range(1, NR):
            cp = pltpu.make_async_remote_copy(
                src_ref=s1, dst_ref=r1.at[k - 1], send_sem=sem.at[0, k - 1], recv_sem=sem.at[1, k - 1],
                device_id={"rows": (r + k) % NR}, device_id_type=MESH)
            cp.start()
            copies.append(cp)
        return copies

    def reduce_frames(copies, s1, r1, s2, r2, sem):
        for cp in copies:
            cp.wait()
        total = s1[...]
        for k in range(NR - 1):
            total += r1[k]
        s2[...] = total
        copies = []
        for k in range(NF - 1):
            cp = pltpu.make_async_remote_copy(
                src_ref=s2, dst_ref=r2.at[k], send_sem=sem.at[0, k], recv_sem=sem.at[1, k],
                device_id={"frames": peer(f, k)}, device_id_type=MESH)
            cp.start()
            copies.append(cp)
        return copies

    def statistics(copies, s2, r2, out):
        for cp in copies:
            cp.wait()
        total = s2[...]
        for k in range(NF - 1):
            total += r2[k]
        count = 64 * 512 * 4
        half = out.shape[1] // 2
        for k in range(2):
            mean = spread_groups(total, k) / count
            square = spread_groups(total, k + 2) / count
            out[0, half * k:half * k + half] = mean
            out[1, half * k:half * k + half] = lax.rsqrt(square - mean * mean + 1e-05)

    for i in range(8):
        for dc in range(2):
            if i < 7 or dc:
                wait_in(pb.at[0, 2], ir.at[2 * i + dc])
    own_inner.wait()
    rows_copies(8, 2, 0, "start")
    lax.fori_loop(0, 16, end_arrival, 0)

    @pl.when(is_end)
    def _():
        own_frame = pltpu.make_async_copy(so.at[3, c, 1 - c], pb.at[chip + c, 1 - c], lsem.at[1])
        own_frame.start()
        own_frame.wait()

    for q in (0, 8):
        pair_rows(q, "start")
    lax.fori_loop(0, 8, early_sums, 0)
    for i, (at, nxt) in enumerate(ENDS):
        add_sums(st_e, E_ROWS * i + 3, at, nxt)
    early_copies = reduce_rows(st_e, s1e, r1e, sem_e1)
    for cp in small[2:]:
        cp.wait()
    fill_weights(ws, w0, w1)
    blocks_not_end(2, 3)
    rows_copies(8, 2, 0, "wait")
    lax.fori_loop(0, 8, edges(2), 0)
    side_copies(0, 8, 2, 0, "start")
    for k, q in enumerate((0, 8)):
        pair_rows(q, "wait")
        edges(0)(q, 0)
        side_copies(q, 1, 0, 4 + 2 * k, "start")
    early_copies = reduce_frames(early_copies, s1e, r1e, s2e, r2e, sem_e2)
    blocks_not_end(3, 4)
    own_pair = pltpu.make_async_copy(so.at[3, c], pb.at[chip + c, pl.ds(0, 2)], lsem.at[1])

    @pl.when(not_end)
    def _():
        own_pair.start()


    lax.fori_loop(0, 8, outer_arrival, 0)

    @pl.when(not_end)
    def _():
        own_pair.wait()
        pair_arrived(chip + c)

    late_copies = reduce_rows(st_l, s1l, r1l, sem_l1)
    pb_copy = pltpu.make_async_copy(pb, pb_out, osem.at[0])
    pb_copy.start()
    side_copies(0, 8, 2, 0, "wait")
    for k, q in enumerate((0, 8)):
        side_copies(q, 1, 0, 4 + 2 * k, "wait")
    for cp in nz_loads:
        cp.wait()
    statistics(early_copies, s2e, r2e, stat_e)

    keeps = border_keeps(f, r)

    def early_conv(q, carry):
        for i, (_, at, nxt) in enumerate(EARLY):
            norm_frame(slot_of(q, at), nxt and slot_of(q, nxt), E_ROWS * q + i, i,
                       pb, tb, ed, stat_e, gain, bias, ea.at[i], ll, None, keeps)
        rows = conv_rows(3, ll, w0, w1)
        for R in range(8):
            for i, (_, at, nxt) in enumerate(EARLY):
                v = pb[q, at[1], R]
                if nxt is not None:
                    v = v + pb[q, nxt[1], R]
                v = v.astype(F32) * (1.0 if nxt is None else 0.5)
                res_e[q, i, R] = (rows[R][i] + v + 0.3 * nz[q, i, R].astype(F32)).astype(BF)
        return carry

    for i, (at, nxt) in enumerate(ENDS):
        norm_frame(at, nxt, E_ROWS * i + 3, i, pb, tb, ed, stat_e, gain, bias, ea.at[i], ll_x, None, keeps)
    rows = conv_rows(5, ll_x, w0, w1)
    for R in range(8):
        for i, (at, nxt) in enumerate(ENDS):
            v = pb[at[0], at[1], R]
            if nxt is not None:
                v = v + pb[nxt[0], nxt[1], R]
            v = v.astype(F32) * (1.0 if nxt is None else 0.5)
            res_x[i, R] = (rows[R][i] + v + 0.3 * nz_x[i, R].astype(F32)).astype(BF)
    lax.fori_loop(0, 4, early_conv, 0)
    late_copies = reduce_frames(late_copies, s1l, r1l, s2l, r2l, sem_l2)
    for q in range(1, 8):
        pair_rows(q, "wait")
    lax.fori_loop(1, 8, edges(0), 0)
    side_copies(1, 7, 0, 2, "start")
    tb_copy = pltpu.make_async_copy(tb, tb_out, osem.at[1])
    tb_copy.start()
    lax.fori_loop(4, 8, early_conv, 0)
    early_copy = pltpu.make_async_copy(res_e, early_out, osem.at[3])
    early_copy.start()
    ends_copy = pltpu.make_async_copy(res_x, ends_out, osem.at[5])
    ends_copy.start()

    for i in range(8):
        inner_copy(i).wait_send()
        inner_send(i, 1).wait_send()
        if i < 7:
            inner_send(i, 0).wait_send()
    for n in range(4):
        outer_part(n, 1, "wait")
        if n != 3:
            outer_part(n, 0, "wait")

    @pl.when(not_end)
    def _():
        for n in range(2):
            halo_copy(n).wait_send()

    for n in range(2, 4):
        @pl.when(is_mid)
        def _():
            detour_copy(n).wait_send()

        @pl.when(jnp.logical_not(is_mid))
        def _():
            halo_copy(n).wait_send()

    @pl.when(is_end)
    def _():
        for n in range(4, 8):
            outer_send(n, 1, True).wait_send()
            outer_send(n, 0, True).wait_send()

    side_copies(1, 7, 0, 2, "wait")
    ed_copy = pltpu.make_async_copy(ed, ed_out, osem.at[2])
    ed_copy.start()
    statistics(late_copies, s2l, r2l, st_out)
    pb_copy.wait()
    tb_copy.wait()
    ed_copy.wait()
    early_copy.wait()
    ends_copy.wait()


def local(video, w_time, w_proj, w_space, gn_gain, gn_bias, noise):
    slots = 2 * NF + 4
    anyw = pl.BlockSpec(memory_space=pl.ANY)
    vm = pl.BlockSpec(memory_space=pltpu.VMEM)
    quads = slots // 4
    dma = pltpu.SemaphoreType.DMA
    gain, bias = gn_gain.reshape(1, 128), gn_bias.reshape(1, 128)
    noise = noise.reshape(8, 8, 8, 32, 128)
    pb, tb, ed, st, early, ends = pl.pallas_call(
        move_kernel,
        out_shape=(
            jax.ShapeDtypeStruct((quads, 4, 8, 32, 128), BF),
            jax.ShapeDtypeStruct((2, quads, 4, 32, 128), BF),
            jax.ShapeDtypeStruct((2, quads, 4, 16, 128), BF),
            jax.ShapeDtypeStruct((2, 8 * L_ROWS, 128), F32),
            jax.ShapeDtypeStruct((8, 3, 8, 32, 128), BF),
            jax.ShapeDtypeStruct((5, 8, 32, 128), BF),
        ),
        in_specs=[anyw, anyw, anyw, anyw, anyw, anyw, anyw],
        out_specs=(anyw, anyw, anyw, vm, anyw, anyw),
        scratch_shapes=[
            pltpu.VMEM((3, 256, 256), BF),
            pltpu.VMEM((256, 128), BF),
            pltpu.VMEM((3, 3, 128, 128), BF),
            pltpu.VMEM((1, 128), F32),
            pltpu.VMEM((1, 128), F32),
            pltpu.VMEM((2, 8, 512, 256), BF),
            pltpu.VMEM((8, 8, 64, 256), BF),
            pltpu.VMEM((4, 2, 8, 64, 256), BF),
            pltpu.VMEM((2, 2, 8, 64, 256), BF),
            pltpu.VMEM((768, 256), BF),
            pltpu.VMEM((8, 2, 8, 32, 128), BF),
            pltpu.VMEM((8, 2, 2, 8, 32, 128), BF),
            pltpu.VMEM((quads, 4, 8, 32, 128), BF),
            pltpu.VMEM((2, quads, 4, 32, 128), BF),
            pltpu.VMEM((2, quads, 4, 16, 128), BF),
            pltpu.VMEM((2, quads, 4, 16, 128), BF),
            pltpu.VMEM((2, 8 * E_ROWS, 128), F32),
            pltpu.VMEM((4 * E_ROWS, 128), F32),
            pltpu.VMEM((NR - 1, 4 * E_ROWS, 128), F32),
            pltpu.VMEM((4 * E_ROWS, 128), F32),
            pltpu.VMEM((NF - 1, 4 * E_ROWS, 128), F32),
            pltpu.VMEM((2, 8 * E_ROWS, 128), F32),
            pltpu.VMEM((2, 8 * L_ROWS, 128), F32),
            pltpu.VMEM((4 * L_ROWS, 128), F32),
            pltpu.VMEM((NR - 1, 4 * L_ROWS, 128), F32),
            pltpu.VMEM((4 * L_ROWS, 128), F32),
            pltpu.VMEM((NF - 1, 4 * L_ROWS, 128), F32),
            pltpu.VMEM((8, 3, 8, 32, 128), BF),
            pltpu.VMEM((768, 256), BF),
            pltpu.VMEM((768, 256), BF),
            pltpu.VMEM((5, 96, 768), BF),
            pltpu.VMEM((5, 2, 16, 128), F32),
            pltpu.VMEM((8, 3, 8, 32, 128), BF),
            pltpu.VMEM((5, 8, 32, 128), BF),
            pltpu.VMEM((5, 160, 768), BF),
            pltpu.VMEM((5, 8, 32, 128), BF),
            dma((2,)),
            dma((8,)), dma((8,)),
            dma((4,)), dma((4,)),
            dma((2,)), dma((2,)),
            dma((16,)), dma((16,)),
            dma((16,)), dma((16,)),
            dma((20,)), dma((20,)),
            dma((8,)), dma((8,)),
            dma((2, NR - 1)), dma((2, NF - 1)),
            dma((2, NR - 1)), dma((2, NF - 1)),
            dma((8,)),
            dma((5,)),
        ],
        compiler_params=pltpu.CompilerParams(collective_id=0, has_side_effects=True, vmem_limit_bytes=60 << 20),
        name="move",
    )(video, w_time, w_proj, w_space, gain, bias, noise)
    out = pl.pallas_call(
        conv_kernel,
        out_shape=jax.ShapeDtypeStruct((64, 8, 32, 128), BF),
        in_specs=[anyw] * 10,
        out_specs=anyw,
        scratch_shapes=[
            pltpu.VMEM((2, 8 * L_ROWS, 128), F32),
            pltpu.VMEM((1, 128), F32),
            pltpu.VMEM((1, 128), F32),
            pltpu.VMEM((quads, 4, 8, 32, 128), BF),
            pltpu.VMEM((2, quads, 4, 32, 128), BF),
            pltpu.VMEM((2, quads, 4, 16, 128), BF),
            pltpu.VMEM((3, 3, 128, 128), BF),
            pltpu.VMEM((8, 5, 8, 32, 128), BF),
            pltpu.VMEM((8, 3, 8, 32, 128), BF),
            *[pltpu.VMEM((5, 8, 32, 128), BF)] * 8,
            pltpu.VMEM((768, 256), BF),
            pltpu.VMEM((768, 256), BF),
            pltpu.VMEM((5, 160, 768), BF),
            pltpu.VMEM((5, 160, 768), BF),
            pltpu.VMEM((5, 8, 32, 128), BF),
            pltpu.VMEM((5, 8, 32, 128), BF),
            pltpu.VMEM((5, 2, 16, 128), F32),
            dma((3, 3)), dma((7,)), dma((7,)), dma((12,)), dma, dma((3,)),
        ],
        compiler_params=pltpu.CompilerParams(vmem_limit_bytes=60 << 20),
        name="conv",
    )(pb, tb, ed, st, early, ends, w_space, gain, bias, noise.reshape(64, 8, 32, 128))
    return out


def solution(mesh):
    in_specs = (
        P("frames", "rows", None, None),
        P(), P(), P(), P(), P(),
        P(None, "rows", "frames", None),
    )
    out_specs = P(None, "rows", "frames", None)
    return jax.shard_map(local, mesh=mesh, in_specs=in_specs, out_specs=out_specs, check_vma=False)
```
